32 devices in a mesh: expert: 4 (over y, x), cuts: 2 (over core), dp: 4 (over z).
Axes of the slice: x: 2, y: 2, z: 4, core: 2. Of those that a mesh axis runs over, the one named last changes fastest.
Arguments:
- activations: bfloat16 [2048, 2048], P(('expert', 'dp')), may hold values from -6 to 6
- out_grad: bfloat16 [2048, 2048], P(('expert', 'dp')), may hold values from -6 to 6
- expert_ids: int32 [2048, 1], P(('expert', 'dp')), may hold values from 0 to 3; in each aligned block of 128 rows (0 to 127, 128 to 255, ...) at most 40 rows name the same one
- gate_up_weight: bfloat16 [4, 2048, 2, 768], P('expert', None, None, 'cuts'), may hold values from -0.125 to 0.125
- down_weight: bfloat16 [4, 2048, 768], P('expert', None, 'cuts'), may hold values from -0.21875 to 0.21875
- master_weight: float32 [4, 2048, 3, 768], P('expert', 'dp', None, 'cuts'), may hold values from -6 to 6
- first_moment: bfloat16 [4, 2048, 3, 768], P('expert', 'dp', None, 'cuts'), may hold values from -6 to 6
- second_moment: bfloat16 [4, 2048, 3, 768], P('expert', 'dp', None, 'cuts'), may hold values from 0.5 to 8
- new_owner: int32 [4, 4], replicated, may hold values from 0 to 3, each once within a row
Outputs:
- input_grad: bfloat16 [2048, 2048], P(('expert', 'dp'), 'cuts')
- moved_master: float32 [4, 4, 512, 3, 768], P('expert', None, 'dp', None, 'cuts')
- moved_first: bfloat16 [4, 4, 512, 3, 768], P('expert', None, 'dp', None, 'cuts')
- moved_second: bfloat16 [4, 4, 512, 3, 768], P('expert', None, 'dp', None, 'cuts')
The draws below stay inside these ranges and needn't reach their ends.
Inputs may be any that keep to these rules, and one draw needn't show every extreme that they name: `expert_ids`: within the 128 rows of one device no expert is named by more than 40 rows, and in every draw some device names some expert exactly 40 times. `new_owner`: each row names every owner index exactly once.
All inputs are finite; a program needn't handle non-finite values.
Results may differ from the reference program's by a relative error of at most 0.019.
Values may be sent and summed in bfloat16 or wider, within the bound.
No kernel may reach another device: no remote copies, remote signals or barrier semaphores. Data moves between devices by JAX's collectives and lax.ppermute only.
A program may use at most 64 MiB of HBM per device.

```python
import math
import jax
import jax.numpy as jnp
import numpy as np
from jax import lax

D = 2048
FF = 768
ROWS_DEV = 128
EXPERTS = 4
CAP = 40
ROWS = 2048
N_EXPERT = 4
N_CUTS = 2
N_DP = 4


def levels(key, dims, shards, least, top_value):
    def one(dim, shards_of):
        heights = jax.random.uniform(jax.random.fold_in(jax.random.fold_in(key, 6), dim), (shards_of,), jnp.float32, least / len(shards), top_value / len(shards))
        return jnp.repeat(jnp.exp(heights), dims[dim] // shards_of).reshape((-1,) + (1,) * (len(dims) - dim - 1))

    loudness = one(*shards[0])
    for cut in shards[1:]:
        loudness = loudness * one(*cut)
    return loudness


def deal_out(own_key, own, number, rows, count, top, most, slope):
    ranking = jax.random.permutation(own_key, count)
    heavy_load, common = portions_of(count, rows * top, most, slope, True), portions_of(count, rows * top, most, slope, False)
    places = jnp.arange(count)

    def named(lengths, offset_by):
        used = int((lengths > 0).sum())
        fixed = max(1, used // 4)
        passed = fixed + (places - fixed + offset_by * (used - fixed)) % max(1, count - fixed)
        return jnp.zeros((count,), jnp.int32).at[ranking[jnp.where(places < fixed, places, passed)]].set(jnp.asarray(lengths, jnp.int32))

    lengths = jnp.where(number % 4 == 0, named(heavy_load, number // 4), named(common, number - number // 4 - 1))
    mixed = jax.random.permutation(jax.random.fold_in(own, 3), count)
    giver, taker = mixed[0:count // 2 * 2:2], mixed[1:count // 2 * 2:2]
    slack = jnp.minimum(lengths[giver] - 1, most - lengths[taker]) // 2
    slack = jnp.where((giver == ranking[0]) | (taker == ranking[0]) | (lengths[taker] == 0), 0, jnp.maximum(slack, 0))
    passed = jax.random.randint(jax.random.fold_in(own, 4), (count // 2,), 0, 1 << 20) % (slack + 1)
    lengths = lengths.at[giver].add(-passed).at[taker].add(passed)
    labels = jnp.searchsorted(jnp.cumsum(lengths), jnp.arange(rows * top), side="right").astype(jnp.int32)
    table = labels.reshape(top, rows).T
    table = table[jax.random.permutation(jax.random.fold_in(own, 1), rows)]
    offset_by = jax.random.randint(jax.random.fold_in(own, 2), (rows, 1), 0, top)
    return jnp.take_along_axis(table, (jnp.arange(top)[None, :] + offset_by) % top, axis=1)


def portions_of(amount, total, reach, slope, full):
    weights = [(1 << 20) // math.isqrt(grade ** slope) + 1 for grade in range(1, amount + 1)]
    largest = reach if full else min(reach, max(-(-total // amount), total * weights[0] // sum(weights)))
    least = 1 if total - largest >= amount - 1 else 0
    holding, surplus = [largest] + [least] * (amount - 1), total - largest - least * (amount - 1)
    while surplus > 0:
        candidates = [i for i in range(1, amount) if holding[i] < largest] or [i for i in range(1, amount) if holding[i] < reach]
        whole, left = sum([weights[i] for i in candidates]), surplus
        for i in candidates:
            more = min(reach - holding[i], max(1, left * weights[i] // whole), surplus)
            holding[i] = holding[i] + more
            surplus = surplus - more
    return np.array(holding)


def noise(key, shape, width, most, cuts=(), held_as=jnp.bfloat16):
    entries = jax.random.normal(key, shape, jnp.float32) * width
    if len(cuts) > 0:
        entries = levels(key, shape, cuts, -0.22, 0.18) * entries
    return jnp.clip(entries, min=-most, max=most).astype(held_as)


def setup_inputs(seed: int = 0) -> dict:
    arg_keys = jax.random.split(jax.random.key(seed), 10)
    activations = noise(arg_keys[0], (ROWS, D), 1.0, 6.0, ((0, 16),))
    out_grad = noise(arg_keys[1], (ROWS, D), 1.0, 6.0, ((0, 16),))
    expert_ids_keys = jax.random.split(jax.random.fold_in(arg_keys[2], 1), ROWS // ROWS_DEV)
    expert_ids_turns = jax.random.permutation(jax.random.fold_in(arg_keys[2], 3), ROWS // ROWS_DEV)
    expert_ids = jax.vmap(lambda own, number: deal_out(jax.random.fold_in(arg_keys[2], 2), own, number, ROWS_DEV, EXPERTS, 1, CAP, 2))(expert_ids_keys, expert_ids_turns).reshape((ROWS, 1))
    gate_up_weight = noise(arg_keys[3], (EXPERTS, D, 2, FF), D ** -0.5, 0.125, ((0, 4), (3, 2)))
    down_weight = noise(arg_keys[4], (EXPERTS, D, FF), FF ** -0.5, 0.21875, ((0, 4), (2, 2)))
    master_weight = noise(arg_keys[5], (EXPERTS, D, 3, FF), 1.0, 6.0, ((0, 4), (1, 4), (3, 2)), jnp.float32)
    first_moment = noise(arg_keys[6], (EXPERTS, D, 3, FF), 1.0, 6.0, ((0, 4), (1, 4), (3, 2)))
    second_moment = jnp.clip(jnp.exp(math.log(8.0) - 2.7725887 * jax.random.uniform(arg_keys[7], (EXPERTS, D, 3, FF), jnp.float32) ** levels(arg_keys[7], (EXPERTS, D, 3, FF), ((0, 4), (1, 4), (3, 2)), -0.2, 0.2)), 0.5, 8.0).astype(jnp.bfloat16)
    new_owner = jax.vmap(lambda own: jax.random.permutation(own, N_EXPERT))(jax.random.split(arg_keys[8], EXPERTS)).reshape((EXPERTS, N_EXPERT)).astype(jnp.int32)
    return {"activations": activations, "out_grad": out_grad, "expert_ids": expert_ids, "gate_up_weight": gate_up_weight, "down_weight": down_weight, "master_weight": master_weight, "first_moment": first_moment, "second_moment": second_moment, "new_owner": new_owner}


beta_first = 0.9
beta_second = 0.95
learn_rate = 0.01
decay_rate = 0.1
epsilon = 1e-08

def route(values, positions):
    experts = positions.shape[0]
    data_count = positions.shape[1]
    source = jnp.arange(experts, dtype=jnp.int32)[:, None, None]
    replica = jnp.arange(data_count, dtype=jnp.int32)[None, :, None]
    filled = jnp.zeros((experts, data_count, experts * CAP, D), jnp.bfloat16)
    filled = filled.at[source, replica, positions].set(values)
    filled = filled.reshape(experts, data_count, experts, CAP, D).transpose(2, 1, 0, 3, 4)
    return filled.reshape(experts, data_count, experts * CAP, D)

def expert_pass(inputs):
    routed_in, routed_grad, gate_up, down = inputs
    features = routed_in.astype(jnp.float32)
    cotangents = routed_grad.astype(jnp.float32)
    gate_matrix = gate_up[:, 0, :].astype(jnp.float32)
    lift_matrix = gate_up[:, 1, :].astype(jnp.float32)
    down_matrix = down.astype(jnp.float32)
    gate_value = jnp.einsum('prd,df->prf', features, gate_matrix)
    lift_value = jnp.einsum('prd,df->prf', features, lift_matrix)
    sigmoid_gate = jax.nn.sigmoid(gate_value)
    silu_gate = gate_value * sigmoid_gate
    hidden = (silu_gate * lift_value).astype(jnp.bfloat16)
    hidden_grad = jnp.einsum('prd,df->prf', cotangents, down_matrix)
    lift_grad = (hidden_grad * silu_gate).astype(jnp.bfloat16)
    gate_grad = (hidden_grad * lift_value * sigmoid_gate * (1.0 + gate_value * (1.0 - sigmoid_gate))).astype(jnp.bfloat16)
    block_width = FF // N_CUTS
    total_grad = jnp.zeros(features.shape, jnp.float32)
    for block_index in range(N_CUTS):
        lower = block_index * block_width
        upper = lower + block_width
        block_grad = jnp.einsum('prf,df->prd', gate_grad[:, :, lower:upper].astype(jnp.float32), gate_matrix[:, lower:upper])
        block_grad = block_grad + jnp.einsum('prf,df->prd', lift_grad[:, :, lower:upper].astype(jnp.float32), lift_matrix[:, lower:upper])
        rounded = lax.optimization_barrier(block_grad.astype(jnp.bfloat16))
        total_grad = total_grad + rounded.astype(jnp.float32)
    gate_part = jnp.einsum('prd,prf->pdf', features, gate_grad.astype(jnp.float32))
    lift_part = jnp.einsum('prd,prf->pdf', features, lift_grad.astype(jnp.float32))
    down_part = jnp.einsum('prd,prf->pdf', cotangents, hidden.astype(jnp.float32))
    stacked = lax.optimization_barrier(jnp.stack([gate_part, lift_part, down_part], axis=2).astype(jnp.bfloat16))
    gradient = lax.optimization_barrier(jnp.sum(stacked.astype(jnp.float32), axis=0)) / N_DP
    return (total_grad.astype(jnp.bfloat16), gradient)

def migrate(tensor, inverse):
    slice_rows = D // (N_EXPERT * N_DP)
    pieces = tensor.reshape(N_EXPERT, N_DP, N_EXPERT, slice_rows, 3, FF)
    picked = jnp.take_along_axis(pieces, inverse[:, None, :, None, None, None], axis=2)
    return picked.transpose(2, 0, 1, 3, 4, 5).reshape(N_EXPERT, N_EXPERT, N_DP * slice_rows, 3, FF)

def reference(activations, out_grad, expert_ids, gate_up_weight, down_weight, master_weight, first_moment, second_moment, new_owner):
    row_expert = expert_ids.reshape(N_EXPERT, N_DP, ROWS_DEV)
    onehot = (row_expert[..., None] == jnp.arange(N_EXPERT, dtype=jnp.int32)).astype(jnp.int32)
    within = lax.optimization_barrier(jnp.sum(jnp.cumsum(onehot, axis=2) * onehot, axis=3)) - 1
    positions = (row_expert * CAP + within).astype(jnp.int32)
    routed_in = route(activations.reshape(N_EXPERT, N_DP, ROWS_DEV, D), positions)
    routed_grad = route(out_grad.reshape(N_EXPERT, N_DP, ROWS_DEV, D), positions)
    slot_grad, gradient = lax.map(expert_pass, (routed_in, routed_grad, gate_up_weight, down_weight))
    slot_grad = slot_grad.reshape(N_EXPERT, N_DP, N_EXPERT, CAP, D)
    source = jnp.arange(N_EXPERT, dtype=jnp.int32)[:, None, None]
    replica = jnp.arange(N_DP, dtype=jnp.int32)[None, :, None]
    input_grad = slot_grad[row_expert, replica, source, within].reshape(ROWS, D)
    first_new = beta_first * first_moment.astype(jnp.float32) + (1.0 - beta_first) * gradient
    second_new = beta_second * second_moment.astype(jnp.float32) + (1.0 - beta_second) * gradient * gradient
    master_new = master_weight - learn_rate * (first_new / (jnp.sqrt(second_new) + epsilon) + decay_rate * master_weight)
    inverse = jnp.argsort(new_owner, axis=1).astype(jnp.int32)
    moved_master = migrate(master_new, inverse)
    moved_first = migrate(first_new.astype(jnp.bfloat16), inverse)
    moved_second = migrate(second_new.astype(jnp.bfloat16), inverse)
    return (input_grad, moved_master, moved_first, moved_second)
```

```python
import functools

import jax
import jax.numpy as jnp
from jax import lax
from jax.experimental import pallas as pl
from jax.experimental.pallas import tpu as pltpu
from jax.sharding import PartitionSpec as P

beta_first = 0.9
beta_second = 0.95
learn_rate = 0.01
decay_rate = 0.1
epsilon = 1e-08

F32 = jnp.float32
BF16 = jnp.bfloat16
VMEM = pl.BlockSpec(memory_space=pltpu.VMEM)
MIB = 1 << 20


def adam_update(master, first_old, second_old, gradient):
    first_new = beta_first * first_old.astype(F32) + (1.0 - beta_first) * gradient
    second_new = beta_second * second_old.astype(F32) + (1.0 - beta_second) * gradient * gradient
    master_new = master - learn_rate * (
        first_new / (jnp.sqrt(second_new) + epsilon) + decay_rate * master
    )
    return (master_new, first_new, second_new)


def expert_grads(gate, lift, hidden_grad):
    sigmoid = jax.nn.sigmoid(gate)
    silu = gate * sigmoid
    hidden = (silu * lift).astype(BF16)
    lift_grad = (hidden_grad * silu).astype(BF16)
    gate_grad = (hidden_grad * lift * sigmoid * (1.0 + gate * (1.0 - sigmoid))).astype(BF16)
    return gate_grad, lift_grad, hidden


def slot_masks(ids, me, experts, capacity):
    rows = ids.shape[1]
    high = max(8, experts)
    match = lax.broadcasted_iota(jnp.int32, (high, rows), 0) == ids
    onehot = jnp.where(match, 1.0, 0.0)
    earlier = jnp.where(
        lax.broadcasted_iota(jnp.int32, (rows, rows), 0)
        < lax.broadcasted_iota(jnp.int32, (rows, rows), 1),
        1.0,
        0.0,
    )
    counts = jnp.dot(onehot.astype(BF16), earlier.astype(BF16), preferred_element_type=F32)
    within = jnp.sum(onehot * counts, axis=0, keepdims=True).astype(jnp.int32)
    slot = lax.broadcasted_iota(jnp.int32, (capacity, rows), 0)
    masks = [
        jnp.where(jnp.where(ids == (me ^ k), within, -1) == slot, 1.0, 0.0) for k in range(experts)
    ]
    return jnp.concatenate(masks, axis=0).astype(BF16)


def dispatch_kernel(experts, capacity, dp_count, ids_ref, in_ref, grad_ref, *out_refs):
    me = lax.axis_index("expert")
    core = lax.axis_index("cuts")
    half = out_refs[0].shape[2] // 2
    cores = in_ref.shape[1] // (dp_count * half)
    masks = slot_masks(ids_ref[...], me, experts, capacity)
    for q in range(dp_count):
        columns = pl.ds(pl.multiple_of((q * cores + core) * half, half), half)
        for x_ref, start in ((in_ref, 0), (grad_ref, half)):
            picked = jnp.dot(masks, x_ref[:, columns], preferred_element_type=F32)
            for k in range(experts):
                out_refs[k][q, :, start : start + half] = picked[
                    k * capacity : (k + 1) * capacity
                ].astype(BF16)


def collect_kernel(experts, dp_count, *refs):
    got, whole, parts = refs[:experts], refs[experts], refs[experts + 1 :]
    me = lax.axis_index("dp")
    for q in range(dp_count):
        joined = jnp.concatenate([got[k][q].astype(F32) for k in range(experts)], axis=0)
        whole[q] = joined.astype(BF16)
    for a in range(1, dp_count):
        parts[a - 1][...] = whole[lax.rem(me + a, dp_count)]


def expert_kernel(dp_count, mine_ref, other_ref, gate_up_ref, down_ref, out_ref):
    core = lax.axis_index("cuts")
    half = mine_ref.shape[2] // 2
    units = down_ref.shape[1]
    rows = mine_ref.shape[1]
    projected = jnp.zeros((rows, 2 * units), F32)
    hidden_grad = jnp.zeros((rows, units), F32)
    for x_ref, side in ((mine_ref, core), (other_ref, 1 - core)):
        for q in range(dp_count):
            depth = pl.ds(pl.multiple_of((2 * q + side) * half, half), half)
            projected += jnp.dot(x_ref[q, :, :half], gate_up_ref[depth, :], preferred_element_type=F32)
            hidden_grad += jnp.dot(x_ref[q, :, half:], down_ref[depth, :], preferred_element_type=F32)
    gate_grad, lift_grad, hidden = expert_grads(
        projected[:, :units], projected[:, units:], hidden_grad
    )
    out_ref[:, :units] = gate_grad
    out_ref[:, units : 2 * units] = lift_grad
    out_ref[:, 2 * units :] = hidden


def slot_grad_kernel(pair_ref, gate_up_ref, keep_ref, send_ref):
    core = lax.axis_index("cuts")
    width = keep_ref.shape[1]
    units = gate_up_ref.shape[1]
    pair = pair_ref[:, :units]
    for out_ref, side in ((keep_ref, core), (send_ref, 1 - core)):
        depth = pl.ds(pl.multiple_of(side * width, width), width)
        out_ref[...] = lax.dot_general(
            pair, gate_up_ref[depth, :], (((1,), (1,)), ((), ())), preferred_element_type=F32
        ).astype(BF16)


def split_kernel(capacity, keep_ref, got_ref, *out_refs):
    total = keep_ref[...].astype(F32) + got_ref[...].astype(F32)
    for k, out_ref in enumerate(out_refs):
        out_ref[...] = total[k * capacity : (k + 1) * capacity].astype(BF16)


def combine_kernel(experts, capacity, ids_ref, *refs):
    got, out_ref = refs[:experts], refs[experts]
    me = lax.axis_index("expert")
    masks = slot_masks(ids_ref[...], me, experts, capacity)
    joined = jnp.concatenate([got[k][...].astype(F32) for k in range(experts)], axis=0)
    out_ref[...] = lax.dot_general(
        masks, joined.astype(BF16), (((0,), (0,)), ((), ())), preferred_element_type=F32
    ).astype(BF16)


def arrange_kernel(experts, owner_ref, master_ref, first_ref, second_ref, *out_refs):
    me = lax.axis_index("expert")
    height = out_refs[0].shape[1]
    for k in range(experts):
        j = 0
        for i in range(experts):
            j = jnp.where(owner_ref[me, i] == (me ^ k), i, j)
        rows = pl.ds(pl.multiple_of(j * height, height), height)
        for m in range(3):
            out_refs[k][m] = master_ref[m, rows, :].astype(BF16)
            out_refs[k][3 + m] = first_ref[m, rows, :]
            out_refs[k][6 + m] = second_ref[m, rows, :]


def weight_kernel(experts, dp_count, owner_ref, *refs):
    mine, other = refs[:dp_count], refs[dp_count : 2 * dp_count]
    hidden = refs[2 * dp_count : 3 * dp_count]
    outs = refs[3 * dp_count : 3 * dp_count + experts]
    held = refs[3 * dp_count + experts]
    me = lax.axis_index("expert")
    core = lax.axis_index("cuts")
    part = lax.axis_index("dp")
    height = outs[0].shape[1]
    units = outs[0].shape[2]
    half = mine[1].shape[1] // 2
    per_half = half // height
    for source, side in ((mine, core), (other, 1 - core)):
        pair = jnp.zeros((half, 2 * units), F32)
        down = jnp.zeros((half, units), F32)
        for a in range(dp_count):
            rows = source[0][part] if a == 0 else source[a][...]
            pair += lax.dot_general(
                rows[:, :half], hidden[a][:, : 2 * units], (((0,), (0,)), ((), ())),
                preferred_element_type=F32,
            )
            down += lax.dot_general(
                rows[:, half:], hidden[a][:, 2 * units :], (((0,), (0,)), ((), ())),
                preferred_element_type=F32,
            )
        pair = pair * (1.0 / dp_count)
        down = down * (1.0 / dp_count)
        for i in range(per_half):
            rows = slice(i * height, (i + 1) * height)
            held[0] = pair[rows, :units].astype(BF16)
            held[1] = pair[rows, units:].astype(BF16)
            held[2] = down[rows].astype(BF16)
            k_of = owner_ref[me, side * per_half + i] ^ me
            for k in range(experts):

                @pl.when(k_of == k)
                def _():
                    outs[k][...] = held[...]


def adam_kernel(source_ref, state_master, state_first, state_second, grad_ref, *refs):
    out_master, out_first, out_second = refs[-3:]
    master, first, second = adam_update(
        state_master[0].astype(F32), state_first[0], state_second[0], grad_ref[0].astype(F32)
    )
    out_master[0, 0] = master
    out_first[0, 0] = first.astype(BF16)
    out_second[0, 0] = second.astype(BF16)


def call(kernel, out_shape, n_in, smem=(), scratch=(), limit=40, flops=0, moved=0):
    specs = [pl.BlockSpec(memory_space=pltpu.SMEM) if i in smem else VMEM for i in range(n_in)]
    return pl.pallas_call(
        kernel,
        out_shape=out_shape,
        in_specs=specs,
        out_specs=jax.tree.map(lambda _: VMEM, out_shape),
        scratch_shapes=list(scratch),
        compiler_params=pltpu.CompilerParams(vmem_limit_bytes=limit * MIB),
        cost_estimate=pl.CostEstimate(flops=flops, bytes_accessed=moved, transcendentals=0),
    )


def shape(*dims, dtype=BF16):
    return jax.ShapeDtypeStruct(dims, dtype)


def adam_step(state, grad, source, buffers, experts):
    parts, height, units = grad.shape
    block = lambda at: pl.BlockSpec((1, height, units), lambda m, s, at=at: (at + m, 0, 0))
    out_block = pl.BlockSpec((1, 1, height, units), lambda m, s: (s[0], m, 0, 0))
    out_shape = [shape(experts, parts, height, units, dtype=t) for t in (F32, BF16, BF16)]
    held = [pl.BlockSpec(memory_space=pl.ANY)] * len(buffers)
    return pl.pallas_call(
        adam_kernel,
        grid_spec=pltpu.PrefetchScalarGridSpec(
            num_scalar_prefetch=1,
            grid=(parts,),
            in_specs=[block(0), block(parts), block(2 * parts), block(0)] + held,
            out_specs=[out_block] * 3,
        ),
        out_shape=out_shape,
        input_output_aliases={5 + i: i for i in range(len(buffers))},
        compiler_params=pltpu.CompilerParams(vmem_limit_bytes=16 * MIB),
        cost_estimate=pl.CostEstimate(
            flops=20 * parts * height * units, bytes_accessed=16 * parts * height * units,
            transcendentals=2 * parts * height * units,
        ),
    )(source, state, state, state, grad, *buffers)


def exchange(tensor, axis, k, count):
    return lax.ppermute(tensor, axis, [(i, i ^ k) for i in range(count)])


def rotate(tensor, axis, a, count):
    return lax.ppermute(tensor, axis, [(i, (i + a) % count) for i in range(count)])


def after(values, *others):
    return lax.optimization_barrier((values, others))[0]


def aligned_local(
    activations,
    out_grad,
    expert_ids,
    gate_up_weight,
    down_weight,
    master_weight,
    first_moment,
    second_moment,
    new_owner,
):
    experts = lax.axis_size("expert")
    dp_count = lax.axis_size("dp")
    cores = lax.axis_size("cuts")
    row_count, model_width = activations.shape
    capacity = row_count // experts + max(1, row_count // (4 * experts))
    slots = experts * capacity
    shard_rows = model_width // dp_count
    half = shard_rows // cores
    height = shard_rows // experts
    units = master_weight.shape[3]
    me = lax.axis_index("expert")
    ids = expert_ids.reshape(1, row_count)
    gate_up = gate_up_weight[0].reshape(model_width, 2 * units)
    down = down_weight[0]

    sent = call(
        functools.partial(dispatch_kernel, experts, capacity, dp_count),
        [shape(dp_count, capacity, 2 * half)] * experts,
        3,
        flops=2 * slots * row_count * model_width,
        moved=4 * row_count * model_width + 4 * slots * model_width,
    )(ids, activations, out_grad)
    got = [sent[0]] + [exchange(sent[k], "expert", k, experts) for k in range(1, experts)]

    states = call(
        functools.partial(arrange_kernel, experts),
        [shape(9, height, units)] * experts,
        4,
        smem=(0,),
        moved=14 * shard_rows * 3 * units,
    )(
        new_owner,
        master_weight[0].transpose(1, 0, 2),
        first_moment[0].transpose(1, 0, 2),
        second_moment[0].transpose(1, 0, 2),
    )

    mine, *parts = call(
        functools.partial(collect_kernel, experts, dp_count),
        [shape(dp_count, slots, 2 * half)] + [shape(slots, 2 * half)] * (dp_count - 1),
        experts,
        moved=12 * slots * model_width,
    )(*got)
    other = exchange(mine, "cuts", 1, cores)
    part_mine = [mine] + [rotate(parts[a - 1], "dp", a, dp_count) for a in range(1, dp_count)]
    states_sent = after(list(states[1:]), *got[1:])
    moved_states = [states[0]] + [
        exchange(states_sent[k - 1], "expert", k, experts) for k in range(1, experts)
    ]

    hidden = call(
        functools.partial(expert_kernel, dp_count),
        shape(slots, 3 * units),
        4,
        flops=6 * slots * model_width * units,
        moved=6 * model_width * units + 8 * slots * model_width,
    )(mine, other, gate_up, down)
    hiddens = [hidden] + [rotate(hidden, "dp", a, dp_count) for a in range(1, dp_count)]
    part_other = [other] + [exchange(part_mine[a], "cuts", 1, cores) for a in range(1, dp_count)]

    keep, give = call(
        slot_grad_kernel,
        [shape(slots, model_width // cores)] * 2,
        2,
        flops=4 * slots * model_width * units,
        moved=4 * model_width * units + 4 * slots * model_width,
    )(hidden, gate_up)
    taken = exchange(give, "cuts", 1, cores)
    back = call(
        functools.partial(split_kernel, capacity),
        [shape(capacity, model_width // cores)] * experts,
        2,
        moved=6 * slots * model_width // cores,
    )(keep, taken)
    returned = [back[0]] + [exchange(back[k], "expert", k, experts) for k in range(1, experts)]
    input_grad = call(
        functools.partial(combine_kernel, experts, capacity),
        shape(row_count, model_width // cores),
        1 + experts,
        flops=2 * slots * row_count * model_width // cores,
        moved=4 * slots * model_width // cores,
    )(ids, *returned)

    grads = call(
        functools.partial(weight_kernel, experts, dp_count),
        [shape(3, height, units)] * experts,
        1 + 3 * dp_count,
        smem=(0,),
        scratch=[pltpu.VMEM((3, height, units), BF16)],
        flops=6 * slots * dp_count * shard_rows * units,
        moved=4 * slots * dp_count * (shard_rows + units),
    )(new_owner, *part_mine, *part_other, *hiddens)
    moved_grads = [grads[0]] + [exchange(grads[k], "expert", k, experts) for k in range(1, experts)]

    buffers = ()
    for k in range(experts):
        source = (me ^ k).astype(jnp.int32).reshape(1)
        buffers = adam_step(moved_states[k], moved_grads[k], source, buffers, experts)
    outs = [b.transpose(0, 2, 1, 3)[None] for b in buffers]
    return (input_grad, *outs)


def plain_local(
    activations,
    out_grad,
    expert_ids,
    gate_up_weight,
    down_weight,
    master_weight,
    first_moment,
    second_moment,
    new_owner,
):
    experts = lax.axis_size("expert")
    dp_count = lax.axis_size("dp")
    row_count = activations.shape[0]
    model_width = activations.shape[1]
    capacity = row_count // experts + max(1, row_count // (4 * experts))
    shard_rows = model_width // dp_count
    slice_rows = shard_rows // experts
    unit_count = master_weight.shape[3]
    expert_index = lax.axis_index("expert")
    owners = lax.dynamic_slice_in_dim(new_owner, expert_index, 1, 0)[0]
    send_order = jnp.argsort(owners)
    scatter = functools.partial(
        lax.all_to_all, axis_name="expert", split_axis=0, concat_axis=0, tiled=True
    )

    def arrange(tensor):
        return jnp.take(tensor.reshape(experts, slice_rows, 3, unit_count), send_order, axis=0)

    early_master = scatter(arrange(master_weight[0]).astype(BF16)).astype(F32)
    early_first = scatter(arrange(first_moment[0]))
    early_second = scatter(arrange(second_moment[0]))
    row_expert = expert_ids[:, 0]
    onehot = (row_expert[:, None] == jnp.arange(experts, dtype=jnp.int32)[None, :]).astype(
        jnp.int32
    )
    within = jnp.sum(jnp.cumsum(onehot, axis=0) * onehot, axis=1) - 1
    target = row_expert * capacity + within
    dispatch = (
        jnp.arange(experts * capacity, dtype=jnp.int32)[:, None] == target[None, :]
    ).astype(BF16)
    rows = jnp.concatenate([activations, out_grad], axis=1)
    sent = jnp.dot(dispatch, rows, preferred_element_type=F32).astype(BF16)
    got = scatter(sent.reshape(experts, capacity, 2 * model_width))
    got = got.reshape(experts * capacity, 2 * model_width)
    slots_in, slots_grad = got[:, :model_width], got[:, model_width:]
    gate_up = gate_up_weight[0].reshape(model_width, -1)
    projected = jnp.dot(slots_in, gate_up, preferred_element_type=F32)
    hidden_grad = jnp.dot(slots_grad, down_weight[0], preferred_element_type=F32)
    gate_grad, lift_grad, hidden = expert_grads(
        projected[:, :unit_count], projected[:, unit_count:], hidden_grad
    )
    pair_grad = jnp.concatenate([gate_grad, lift_grad], axis=1)
    slot_grad = lax.dot_general(
        pair_grad, gate_up, (((1,), (1,)), ((), ())), preferred_element_type=F32
    )
    returned = scatter(slot_grad.astype(BF16).reshape(experts, capacity, model_width))
    row_grad = lax.dot_general(
        dispatch,
        returned.reshape(experts * capacity, model_width),
        (((0,), (0,)), ((), ())),
        preferred_element_type=F32,
    )
    input_grad = lax.psum_scatter(row_grad.astype(BF16), "cuts", scatter_dimension=1, tiled=True)
    paired = lax.dot_general(
        slots_in, pair_grad, (((0,), (0,)), ((), ())), preferred_element_type=F32
    )
    downed = lax.dot_general(
        slots_grad, hidden, (((0,), (0,)), ((), ())), preferred_element_type=F32
    )
    summed = lax.psum_scatter(
        jnp.concatenate([paired, downed], axis=1).astype(BF16),
        "dp",
        scatter_dimension=0,
        tiled=True,
    ).astype(F32)
    gradient = summed.reshape(shard_rows, 3, unit_count) / dp_count
    moved_gradient = scatter(arrange(gradient).astype(BF16)).astype(F32)
    moved_master, first_new, second_new = adam_update(
        early_master, early_first, early_second, moved_gradient
    )
    return (
        input_grad,
        moved_master[None],
        first_new.astype(BF16)[None],
        second_new.astype(BF16)[None],
    )


def local(*args):
    experts = lax.axis_size("expert")
    dp_count = lax.axis_size("dp")
    cores = lax.axis_size("cuts")
    row_count, model_width = args[0].shape
    capacity = row_count // experts + max(1, row_count // (4 * experts))
    height = model_width // (dp_count * experts)
    whole_tiles = (
        experts & (experts - 1) == 0
        and cores == 2
        and capacity % 8 == 0
        and (experts * capacity) % 16 == 0
        and row_count % 128 == 0
        and height % 128 == 0
        and (model_width // (dp_count * cores)) % height == 0
        and args[5].shape[3] % 128 == 0
    )
    return (aligned_local if whole_tiles else plain_local)(*args)


def solution(mesh):
    in_specs = (
        P(("expert", "dp"), None),
        P(("expert", "dp"), None),
        P(("expert", "dp"), None),
        P("expert", None, None, "cuts"),
        P("expert", None, "cuts"),
        P("expert", "dp", None, "cuts"),
        P("expert", "dp", None, "cuts"),
        P("expert", "dp", None, "cuts"),
        P(),
    )
    out_specs = (
        P(("expert", "dp"), "cuts"),
        P("expert", None, "dp", None, "cuts"),
        P("expert", None, "dp", None, "cuts"),
        P("expert", None, "dp", None, "cuts"),
    )
    return jax.shard_map(local, mesh=mesh, in_specs=in_specs, out_specs=out_specs, check_vma=False)
```

```python
import functools

import jax
import jax.numpy as jnp
from jax import lax
from jax.experimental import pallas as pl
from jax.experimental.pallas import tpu as pltpu
from jax.sharding import PartitionSpec as P

beta_first = 0.9
beta_second = 0.95
learn_rate = 0.01
decay_rate = 0.1
epsilon = 1e-08

F32 = jnp.float32
BF16 = jnp.bfloat16
VMEM = pl.BlockSpec(memory_space=pltpu.VMEM)
SMEM = pl.BlockSpec(memory_space=pltpu.SMEM)
HBM = pl.BlockSpec(memory_space=pltpu.HBM)
MIB = 1 << 20


def adam_update(master, first_old, second_old, gradient):
    first_new = beta_first * first_old.astype(F32) + (1.0 - beta_first) * gradient
    second_new = beta_second * second_old.astype(F32) + (1.0 - beta_second) * gradient * gradient
    master_new = master - learn_rate * (
        first_new / (jnp.sqrt(second_new) + epsilon) + decay_rate * master
    )
    return (master_new, first_new, second_new)


def expert_grads(gate, lift, hidden_grad):
    sigmoid = jax.nn.sigmoid(gate)
    silu = gate * sigmoid
    hidden = (silu * lift).astype(BF16)
    lift_grad = (hidden_grad * silu).astype(BF16)
    gate_grad = (hidden_grad * lift * sigmoid * (1.0 + gate * (1.0 - sigmoid))).astype(BF16)
    return gate_grad, lift_grad, hidden


def slot_masks(ids, me, experts, capacity):
    rows = ids.shape[1]
    high = max(8, experts)
    match = lax.broadcasted_iota(jnp.int32, (high, rows), 0) == ids
    onehot = jnp.where(match, 1.0, 0.0)
    earlier = jnp.where(
        lax.broadcasted_iota(jnp.int32, (rows, rows), 0)
        < lax.broadcasted_iota(jnp.int32, (rows, rows), 1),
        1.0,
        0.0,
    )
    counts = jnp.dot(onehot.astype(BF16), earlier.astype(BF16), preferred_element_type=F32)
    within = jnp.sum(onehot * counts, axis=0, keepdims=True).astype(jnp.int32)
    slot = lax.broadcasted_iota(jnp.int32, (capacity, rows), 0)
    masks = [
        jnp.where(jnp.where(ids == (me ^ k), within, -1) == slot, 1.0, 0.0) for k in range(experts)
    ]
    return jnp.concatenate(masks, axis=0).astype(BF16)


def dispatch_kernel(experts, capacity, dp_count, ids_any, in_any, grad_any, *refs):
    outs, (ids_ref, held, sems) = refs[:experts], refs[experts:]
    me = lax.axis_index("expert")
    core = lax.axis_index("cuts")
    half = held.shape[3]
    cores = in_any.shape[1] // (dp_count * half)
    first = pltpu.make_async_copy(ids_any, ids_ref, sems.at[2 * dp_count])
    first.start()
    copies = []
    for x, x_any in enumerate((in_any, grad_any)):
        for q in range(dp_count):
            columns = pl.ds(pl.multiple_of((q * cores + core) * half, half), half)
            copies.append(
                pltpu.make_async_copy(x_any.at[:, columns], held.at[x, q], sems.at[x * dp_count + q])
            )
            copies[-1].start()
    first.wait()
    masks = slot_masks(ids_ref[...], me, experts, capacity)
    for x in range(2):
        for q in range(dp_count):
            copies[x * dp_count + q].wait()
            picked = jnp.dot(masks, held[x, q], preferred_element_type=F32)
            for k in range(experts):
                outs[k][q, :, x * half : (x + 1) * half] = picked[
                    k * capacity : (k + 1) * capacity
                ].astype(BF16)


def collect_kernel(experts, dp_count, *refs):
    got, whole, parts = refs[:experts], refs[experts], refs[experts + 1 :]
    part = lax.axis_index("dp")
    for q in range(dp_count):
        joined = jnp.concatenate([got[k][q].astype(F32) for k in range(experts)], axis=0)
        whole[q] = joined.astype(BF16)
    for k in range(1, dp_count):
        parts[k - 1][...] = whole[part ^ k]


def expert_kernel(dp_count, mine_ref, other_ref, gate_up_ref, down_ref, out_ref):
    core = lax.axis_index("cuts")
    half = mine_ref.shape[2] // 2
    units = down_ref.shape[1]
    rows = mine_ref.shape[1]
    projected = jnp.zeros((rows, 2 * units), F32)
    hidden_grad = jnp.zeros((rows, units), F32)
    for x_ref, side in ((mine_ref, core), (other_ref, 1 - core)):
        for q in range(dp_count):
            depth = pl.ds(pl.multiple_of((2 * q + side) * half, half), half)
            projected += jnp.dot(x_ref[q, :, :half], gate_up_ref[depth, :], preferred_element_type=F32)
            hidden_grad += jnp.dot(x_ref[q, :, half:], down_ref[depth, :], preferred_element_type=F32)
    gate_grad, lift_grad, hidden = expert_grads(
        projected[:, :units], projected[:, units:], hidden_grad
    )
    out_ref[:, :units] = gate_grad
    out_ref[:, units : 2 * units] = lift_grad
    out_ref[:, 2 * units :] = hidden


def slot_grad_kernel(pair_ref, gate_up_ref, keep_ref, send_ref):
    core = lax.axis_index("cuts")
    width = keep_ref.shape[1]
    units = gate_up_ref.shape[1]
    pair = pair_ref[:, :units]
    for out_ref, side in ((keep_ref, core), (send_ref, 1 - core)):
        depth = pl.ds(pl.multiple_of(side * width, width), width)
        out_ref[...] = lax.dot_general(
            pair, gate_up_ref[depth, :], (((1,), (1,)), ((), ())), preferred_element_type=F32
        ).astype(BF16)


def split_kernel(capacity, keep_ref, got_ref, *out_refs):
    total = keep_ref[...].astype(F32) + got_ref[...].astype(F32)
    for k, out_ref in enumerate(out_refs):
        out_ref[...] = total[k * capacity : (k + 1) * capacity].astype(BF16)


def combine_kernel(experts, capacity, ids_any, *refs):
    got, (out_ref, ids_ref, sem) = refs[:experts], refs[experts:]
    me = lax.axis_index("expert")
    copy = pltpu.make_async_copy(ids_any, ids_ref, sem)
    copy.start()
    copy.wait()
    masks = slot_masks(ids_ref[...], me, experts, capacity)
    joined = jnp.concatenate([got[k][...].astype(F32) for k in range(experts)], axis=0)
    out_ref[...] = lax.dot_general(
        masks, joined.astype(BF16), (((0,), (0,)), ((), ())), preferred_element_type=F32
    ).astype(BF16)


def slice_for(owner_ref, me, target, experts):
    j = 0
    for i in range(experts):
        j = jnp.where(owner_ref[me, i] == target, i, j)
    return j


def arrange_kernel(experts, groups, owner_ref, master_any, first_any, second_any, *refs):
    outs, (held, sems) = refs[: len(groups)], refs[len(groups) :]
    me = lax.axis_index("expert")
    height = held.shape[2]
    stored = (master_any, first_any, second_any)
    masters, others = [], []
    for g, (k, parts) in enumerate(groups):
        j = slice_for(owner_ref, me, me ^ k, experts)
        rows = pl.ds(pl.multiple_of(j * height, height), height)
        for n, i in enumerate(parts):
            target = held.at[k] if i == 0 else outs[g].at[pl.ds(3 * n, 3)]
            copy = pltpu.make_async_copy(stored[i].at[:, rows, :], target, sems.at[k, i])
            copy.start()
            if i == 0:
                masters.append((copy, k, g, n))
            else:
                others.append(copy)
    for copy, k, g, n in masters:
        copy.wait()
        for m in range(3):
            outs[g][3 * n + m] = held[k, m].astype(BF16)
    for copy in others:
        copy.wait()


def weight_kernel(experts, dp_count, owner_ref, *refs):
    mine, other = refs[:dp_count], refs[dp_count : 2 * dp_count]
    hidden = refs[2 * dp_count : 3 * dp_count]
    outs = refs[3 * dp_count : 3 * dp_count + experts]
    rows_ref, hidden_ref, held = refs[3 * dp_count + experts :]
    me = lax.axis_index("expert")
    core = lax.axis_index("cuts")
    part = lax.axis_index("dp")
    height = outs[0].shape[1]
    units = outs[0].shape[2]
    slots = hidden[0].shape[0]
    half = mine[0].shape[2] // 2
    per_half = half // height
    for k in range(dp_count):
        hidden_ref[k * slots : (k + 1) * slots] = hidden[k][...]
    for source, side in ((mine, core), (other, 1 - core)):
        rows_ref[:slots] = source[0][part]
        for a in range(1, dp_count):
            rows_ref[a * slots : (a + 1) * slots] = source[a][...]
        sums = [
            lax.dot_general(
                rows_ref[:, at : at + half], hidden_ref[:, low:high], (((0,), (0,)), ((), ())),
                preferred_element_type=F32,
            )
            * (1.0 / dp_count)
            for at, low, high in (
                (0, 0, units), (0, units, 2 * units), (half, 2 * units, 3 * units),
            )
        ]
        for i in range(per_half):
            for m in range(3):
                held[m] = sums[m][i * height : (i + 1) * height].astype(BF16)
            k_of = owner_ref[me, side * per_half + i] ^ me
            for k in range(experts):

                @pl.when(k_of == k)
                def _():
                    outs[k][...] = held[...]


def adam_kernel(k, places, grad_ref, *refs):
    outs, held, sems = refs[-7:-4], refs[-4:-1], refs[-1]
    block = lax.axis_index("expert") ^ k
    copies = []
    for m in range(3):
        master, first, second = [refs[ref][3 * n + m] for ref, n in places]
        values = adam_update(master.astype(F32), first, second, grad_ref[m].astype(F32))
        for i in range(3):
            held[i][m] = values[i].astype(held[i].dtype)
            copies.append(
                pltpu.make_async_copy(held[i].at[m], outs[i].at[block, m], sems.at[m, i])
            )
            copies[-1].start()
    for copy in copies:
        copy.wait()


def call(kernel, out_shape, n_in, smem=(), held=(), scratch=(), limit=16, flops=0, moved=0):
    specs = [
        SMEM if i in smem else HBM if i in held else VMEM
        for i in range(n_in)
    ]
    return pl.pallas_call(
        kernel,
        out_shape=out_shape,
        in_specs=specs,
        out_specs=jax.tree.map(lambda _: VMEM, out_shape),
        scratch_shapes=list(scratch),
        compiler_params=pltpu.CompilerParams(vmem_limit_bytes=limit * MIB),
        cost_estimate=pl.CostEstimate(flops=flops, bytes_accessed=moved, transcendentals=0),
    )


def shape(*dims, dtype=BF16):
    return jax.ShapeDtypeStruct(dims, dtype)


def adam_step(states, places, grad, k, buffers, experts):
    parts, height, units = grad.shape
    types = (F32, BF16, BF16)
    return pl.pallas_call(
        functools.partial(adam_kernel, k, places),
        out_shape=[shape(experts, parts, height, units, dtype=t) for t in types],
        in_specs=[VMEM] * (1 + len(states)) + [HBM] * len(buffers),
        out_specs=[HBM] * 3,
        scratch_shapes=[pltpu.VMEM((parts, height, units), t) for t in types]
        + [pltpu.SemaphoreType.DMA((parts, 3))],
        input_output_aliases={1 + len(states) + i: i for i in range(len(buffers))},
        compiler_params=pltpu.CompilerParams(vmem_limit_bytes=16 * MIB),
        cost_estimate=pl.CostEstimate(
            flops=20 * parts * height * units,
            bytes_accessed=16 * parts * height * units,
            transcendentals=2 * parts * height * units,
        ),
    )(grad, *states, *buffers)


def exchange(tensor, axis, k, count):
    return lax.ppermute(tensor, axis, [(i, i ^ k) for i in range(count)])


def after(values, *others):
    return lax.optimization_barrier((values, others))[0]


def aligned_local(
    activations,
    out_grad,
    expert_ids,
    gate_up_weight,
    down_weight,
    master_weight,
    first_moment,
    second_moment,
    new_owner,
):
    experts = lax.axis_size("expert")
    dp_count = lax.axis_size("dp")
    cores = lax.axis_size("cuts")
    row_count, model_width = activations.shape
    capacity = row_count // experts + max(1, row_count // (4 * experts))
    slots = experts * capacity
    shard_rows = model_width // dp_count
    half = shard_rows // cores
    height = shard_rows // experts
    units = master_weight.shape[3]
    ids = expert_ids.reshape(1, row_count)
    gate_up = gate_up_weight[0].reshape(model_width, 2 * units)
    down = down_weight[0]

    sent = call(
        functools.partial(dispatch_kernel, experts, capacity, dp_count),
        [shape(dp_count, capacity, 2 * half)] * experts,
        3,
        held=(0, 1, 2),
        scratch=[
            pltpu.VMEM((1, row_count), jnp.int32),
            pltpu.VMEM((2, dp_count, row_count, half), BF16),
            pltpu.SemaphoreType.DMA((2 * dp_count + 1,)),
        ],
        flops=2 * slots * row_count * model_width,
        moved=2 * row_count * model_width + 4 * slots * model_width,
    )(ids, activations, out_grad)
    got = [sent[0]] + [exchange(sent[k], "expert", k, experts) for k in range(1, experts)]

    near = [k for k in range(1, experts) if k.bit_count() == 1]
    far = [k for k in range(1, experts) if k.bit_count() > 1]
    groups = [(k, (0, 1, 2)) for k in range(experts)]
    stored = [t[0].transpose(1, 0, 2) for t in (master_weight, first_moment, second_moment)]
    states = call(
        functools.partial(arrange_kernel, experts, groups),
        [shape(3 * len(parts), height, units) for _, parts in groups],
        4,
        smem=(0,),
        held=(1, 2, 3),
        scratch=[
            pltpu.VMEM((experts, 3, height, units), F32),
            pltpu.SemaphoreType.DMA((experts, 3)),
        ],
        moved=14 * shard_rows * 3 * units,
    )(new_owner, *stored)
    got, states = lax.optimization_barrier((got, states))
    states = dict(zip(groups, states))

    def send_states(parts, ks, *others):
        for k in ks:
            states[k, parts] = exchange(after(states[k, parts], *others), "expert", k, experts)
        return [states[k, parts] for k in ks]

    mine, *parts = call(
        functools.partial(collect_kernel, experts, dp_count),
        [shape(dp_count, slots, 2 * half)] + [shape(slots, 2 * half)] * (dp_count - 1),
        experts,
        moved=12 * slots * model_width,
    )(*got)
    other = exchange(mine, "cuts", 1, cores)
    rows = {1: exchange(parts[0], "dp", 1, dp_count)}
    sent_states = send_states((0, 1, 2), near)

    hidden = call(
        functools.partial(expert_kernel, dp_count),
        shape(slots, 3 * units),
        4,
        flops=6 * slots * model_width * units,
        moved=6 * model_width * units + 8 * slots * model_width,
    )(mine, other, gate_up, down)

    hiddens = {0: hidden}
    for bits in range(1, dp_count.bit_length()):
        level = [k for k in range(dp_count - 1, 0, -1) if k.bit_count() == bits]
        for k in level:
            low = k & -k
            block = hiddens[k ^ low]
            if bits > 1:
                block = after(block, tied)
            elif k == 1:
                block = after(block, rows[1])
            hiddens[k] = exchange(block, "dp", low, dp_count)
        if bits == 1:
            send_states((0, 1, 2), far, hidden, sent_states)
        else:
            for k in range(2, dp_count):
                if k not in rows:
                    rows[k] = exchange(after(parts[k - 1], tied), "dp", k, dp_count)
        tied = [hiddens[k] for k in level]
    hiddens = [hiddens[k] for k in range(dp_count)]
    rows_mine = [mine] + [rows[k] for k in range(1, dp_count)]
    rows_other = [other] + [exchange(rows[k], "cuts", 1, cores) for k in range(1, dp_count)]

    keep, give = call(
        slot_grad_kernel,
        [shape(slots, model_width // cores)] * 2,
        2,
        flops=4 * slots * model_width * units,
        moved=4 * model_width * units + 4 * slots * model_width,
    )(hidden, gate_up)
    taken = exchange(give, "cuts", 1, cores)
    back = call(
        functools.partial(split_kernel, capacity),
        [shape(capacity, model_width // cores)] * experts,
        2,
        moved=6 * slots * model_width // cores,
    )(keep, taken)
    returned = [back[0]] + [exchange(back[k], "expert", k, experts) for k in range(1, experts)]
    input_grad = call(
        functools.partial(combine_kernel, experts, capacity),
        shape(row_count, model_width // cores),
        1 + experts,
        held=(0,),
        scratch=[pltpu.VMEM((1, row_count), jnp.int32), pltpu.SemaphoreType.DMA(())],
        flops=2 * slots * row_count * model_width // cores,
        moved=4 * slots * model_width // cores,
    )(ids, *returned)

    grads = call(
        functools.partial(weight_kernel, experts, dp_count),
        [shape(3, height, units)] * experts,
        1 + 3 * dp_count,
        smem=(0,),
        scratch=[
            pltpu.VMEM((slots * dp_count, 2 * half), BF16),
            pltpu.VMEM((slots * dp_count, 3 * units), BF16),
            pltpu.VMEM((3, height, units), BF16),
        ],
        flops=6 * slots * dp_count * shard_rows * units,
        moved=4 * slots * dp_count * (shard_rows + units),
    )(new_owner, *rows_mine, *rows_other, *hiddens)
    moved_grads = {0: grads[0]}
    for k in near + far:
        grad = after(grads[k], returned) if k in far else grads[k]
        moved_grads[k] = exchange(grad, "expert", k, experts)

    buffers = ()
    for k in range(experts):
        held = [group for group in groups if group[0] == k]
        places = [
            next((n, group[1].index(i)) for n, group in enumerate(held) if i in group[1])
            for i in range(3)
        ]
        buffers = adam_step(
            [states[group] for group in held], places, moved_grads[k], k, buffers, experts
        )
    outs = [b.transpose(0, 2, 1, 3)[None] for b in buffers]
    return (input_grad, *outs)


def plain_local(
    activations,
    out_grad,
    expert_ids,
    gate_up_weight,
    down_weight,
    master_weight,
    first_moment,
    second_moment,
    new_owner,
):
    experts = lax.axis_size("expert")
    dp_count = lax.axis_size("dp")
    row_count = activations.shape[0]
    model_width = activations.shape[1]
    capacity = row_count // experts + max(1, row_count // (4 * experts))
    shard_rows = model_width // dp_count
    slice_rows = shard_rows // experts
    unit_count = master_weight.shape[3]
    expert_index = lax.axis_index("expert")
    owners = lax.dynamic_slice_in_dim(new_owner, expert_index, 1, 0)[0]
    send_order = jnp.argsort(owners)
    scatter = functools.partial(
        lax.all_to_all, axis_name="expert", split_axis=0, concat_axis=0, tiled=True
    )

    def arrange(tensor):
        return jnp.take(tensor.reshape(experts, slice_rows, 3, unit_count), send_order, axis=0)

    early_master = scatter(arrange(master_weight[0]).astype(BF16)).astype(F32)
    early_first = scatter(arrange(first_moment[0]))
    early_second = scatter(arrange(second_moment[0]))
    row_expert = expert_ids[:, 0]
    onehot = (row_expert[:, None] == jnp.arange(experts, dtype=jnp.int32)[None, :]).astype(
        jnp.int32
    )
    within = jnp.sum(jnp.cumsum(onehot, axis=0) * onehot, axis=1) - 1
    target = row_expert * capacity + within
    dispatch = (
        jnp.arange(experts * capacity, dtype=jnp.int32)[:, None] == target[None, :]
    ).astype(BF16)
    rows = jnp.concatenate([activations, out_grad], axis=1)
    sent = jnp.dot(dispatch, rows, preferred_element_type=F32).astype(BF16)
    got = scatter(sent.reshape(experts, capacity, 2 * model_width))
    got = got.reshape(experts * capacity, 2 * model_width)
    slots_in, slots_grad = got[:, :model_width], got[:, model_width:]
    gate_up = gate_up_weight[0].reshape(model_width, -1)
    projected = jnp.dot(slots_in, gate_up, preferred_element_type=F32)
    hidden_grad = jnp.dot(slots_grad, down_weight[0], preferred_element_type=F32)
    gate_grad, lift_grad, hidden = expert_grads(
        projected[:, :unit_count], projected[:, unit_count:], hidden_grad
    )
    pair_grad = jnp.concatenate([gate_grad, lift_grad], axis=1)
    slot_grad = lax.dot_general(
        pair_grad, gate_up, (((1,), (1,)), ((), ())), preferred_element_type=F32
    )
    returned = scatter(slot_grad.astype(BF16).reshape(experts, capacity, model_width))
    row_grad = lax.dot_general(
        dispatch,
        returned.reshape(experts * capacity, model_width),
        (((0,), (0,)), ((), ())),
        preferred_element_type=F32,
    )
    input_grad = lax.psum_scatter(row_grad.astype(BF16), "cuts", scatter_dimension=1, tiled=True)
    paired = lax.dot_general(
        slots_in, pair_grad, (((0,), (0,)), ((), ())), preferred_element_type=F32
    )
    downed = lax.dot_general(
        slots_grad, hidden, (((0,), (0,)), ((), ())), preferred_element_type=F32
    )
    summed = lax.psum_scatter(
        jnp.concatenate([paired, downed], axis=1).astype(BF16),
        "dp",
        scatter_dimension=0,
        tiled=True,
    ).astype(F32)
    gradient = summed.reshape(shard_rows, 3, unit_count) / dp_count
    moved_gradient = scatter(arrange(gradient).astype(BF16)).astype(F32)
    moved_master, first_new, second_new = adam_update(
        early_master, early_first, early_second, moved_gradient
    )
    return (
        input_grad,
        moved_master[None],
        first_new.astype(BF16)[None],
        second_new.astype(BF16)[None],
    )


def local(*args):
    experts = lax.axis_size("expert")
    dp_count = lax.axis_size("dp")
    cores = lax.axis_size("cuts")
    row_count, model_width = args[0].shape
    capacity = row_count // experts + max(1, row_count // (4 * experts))
    height = model_width // (dp_count * experts)
    whole_tiles = (
        experts & (experts - 1) == 0
        and dp_count & (dp_count - 1) == 0
        and cores == 2
        and capacity % 8 == 0
        and (experts * capacity) % 16 == 0
        and row_count % 128 == 0
        and height % 128 == 0
        and (model_width // (dp_count * cores)) % height == 0
        and args[5].shape[3] % 128 == 0
    )
    return (aligned_local if whole_tiles else plain_local)(*args)


def solution(mesh):
    in_specs = (
        P(("expert", "dp"), None),
        P(("expert", "dp"), None),
        P(("expert", "dp"), None),
        P("expert", None, None, "cuts"),
        P("expert", None, "cuts"),
        P("expert", "dp", None, "cuts"),
        P("expert", "dp", None, "cuts"),
        P("expert", "dp", None, "cuts"),
        P(),
    )
    out_specs = (
        P(("expert", "dp"), "cuts"),
        P("expert", None, "dp", None, "cuts"),
        P("expert", None, "dp", None, "cuts"),
        P("expert", None, "dp", None, "cuts"),
    )
    return jax.shard_map(local, mesh=mesh, in_specs=in_specs, out_specs=out_specs, check_vma=False)
```

```python
import functools

import jax
import jax.numpy as jnp
from jax import lax
from jax.experimental import pallas as pl
from jax.experimental.pallas import tpu as pltpu
from jax.sharding import PartitionSpec as P

beta_first = 0.9
beta_second = 0.95
learn_rate = 0.01
decay_rate = 0.1
epsilon = 1e-08

F32 = jnp.float32
BF16 = jnp.bfloat16
VMEM = pl.BlockSpec(memory_space=pltpu.VMEM)
SMEM = pl.BlockSpec(memory_space=pltpu.SMEM)
HBM = pl.BlockSpec(memory_space=pltpu.HBM)
MIB = 1 << 20
DISPATCH_LIMIT = 60
PASS_FLOPS = 4 * 10**9


def adam_update(master, first_old, second_old, gradient):
    first_new = beta_first * first_old.astype(F32) + (1.0 - beta_first) * gradient
    second_new = beta_second * second_old.astype(F32) + (1.0 - beta_second) * gradient * gradient
    master_new = master - learn_rate * (
        first_new / (jnp.sqrt(second_new) + epsilon) + decay_rate * master
    )
    return (master_new, first_new, second_new)


def expert_grads(gate, lift, hidden_grad):
    sigmoid = jax.nn.sigmoid(gate)
    silu = gate * sigmoid
    hidden = (silu * lift).astype(BF16)
    lift_grad = (hidden_grad * silu).astype(BF16)
    gate_grad = (hidden_grad * lift * sigmoid * (1.0 + gate * (1.0 - sigmoid))).astype(BF16)
    return gate_grad, lift_grad, hidden


def slot_masks(ids, me, experts, capacity):
    rows = ids.shape[1]
    high = max(8, experts)
    match = lax.broadcasted_iota(jnp.int32, (high, rows), 0) == ids
    onehot = jnp.where(match, 1.0, 0.0)
    earlier = jnp.where(
        lax.broadcasted_iota(jnp.int32, (rows, rows), 0)
        < lax.broadcasted_iota(jnp.int32, (rows, rows), 1),
        1.0,
        0.0,
    )
    counts = jnp.dot(onehot.astype(BF16), earlier.astype(BF16), preferred_element_type=F32)
    within = jnp.sum(onehot * counts, axis=0, keepdims=True).astype(jnp.int32)
    slot = lax.broadcasted_iota(jnp.int32, (capacity, rows), 0)
    masks = [
        jnp.where(jnp.where(ids == (me ^ k), within, -1) == slot, 1.0, 0.0) for k in range(experts)
    ]
    return jnp.concatenate(masks, axis=0).astype(BF16)


def dispatch_kernel(experts, capacity, dp_count, ids_any, in_any, grad_any, *refs):
    outs, (masks_ref, ids_ref, held, sems) = refs[:experts], refs[experts:]
    me = lax.axis_index("expert")
    core = lax.axis_index("cuts")
    half = outs[0].shape[2] // 2
    cores = in_any.shape[1] // (dp_count * half)
    first = pltpu.make_async_copy(ids_any, ids_ref, sems.at[2])
    first.start()
    copies = [
        pltpu.make_async_copy(x_any, held.at[x], sems.at[x])
        for x, x_any in enumerate((in_any, grad_any))
    ]
    for copy in copies:
        copy.start()
    first.wait()
    masks = slot_masks(ids_ref[...], me, experts, capacity)
    masks_ref[...] = masks
    for x in range(2):
        copies[x].wait()
        for q in range(dp_count):
            columns = pl.ds(pl.multiple_of((q * cores + core) * half, half), half)
            picked = jnp.dot(masks, held[x, :, columns], preferred_element_type=F32)
            for k in range(experts):
                outs[k][q, :, x * half : (x + 1) * half] = picked[
                    k * capacity : (k + 1) * capacity
                ].astype(BF16)


def collect_kernel(experts, dp_count, *refs):
    got, whole, parts = refs[:experts], refs[experts], refs[experts + 1 :]
    part = lax.axis_index("dp")
    for q in range(dp_count):
        joined = jnp.concatenate([got[k][q].astype(F32) for k in range(experts)], axis=0)
        whole[q] = joined.astype(BF16)
    for k in range(1, dp_count):
        parts[k - 1][...] = whole[part ^ k]


def expert_kernel(dp_count, mine_ref, other_ref, gate_up_ref, down_ref, out_ref):
    core = lax.axis_index("cuts")
    half = mine_ref.shape[2] // 2
    units = down_ref.shape[1]
    rows = mine_ref.shape[1]
    projected = jnp.zeros((rows, 2 * units), F32)
    hidden_grad = jnp.zeros((rows, units), F32)
    for x_ref, side in ((mine_ref, core), (other_ref, 1 - core)):
        for q in range(dp_count):
            depth = pl.ds(pl.multiple_of((2 * q + side) * half, half), half)
            projected += jnp.dot(x_ref[q, :, :half], gate_up_ref[depth, :], preferred_element_type=F32)
            hidden_grad += jnp.dot(x_ref[q, :, half:], down_ref[depth, :], preferred_element_type=F32)
    gate_grad, lift_grad, hidden = expert_grads(
        projected[:, :units], projected[:, units:], hidden_grad
    )
    out_ref[:, :units] = gate_grad
    out_ref[:, units : 2 * units] = lift_grad
    out_ref[:, 2 * units :] = hidden


def pass_kernel(got_ref, out_ref):
    out_ref[...] = got_ref[...]


def slot_grad_kernel(pair_ref, gate_up_ref, keep_ref, send_ref):
    core = lax.axis_index("cuts")
    width = keep_ref.shape[1]
    units = gate_up_ref.shape[1]
    pair = pair_ref[:, :units]
    for out_ref, side in ((keep_ref, core), (send_ref, 1 - core)):
        depth = pl.ds(pl.multiple_of(side * width, width), width)
        out_ref[...] = lax.dot_general(
            pair, gate_up_ref[depth, :], (((1,), (1,)), ((), ())), preferred_element_type=F32
        ).astype(BF16)


def split_kernel(experts, capacity, carriers, keep_ref, got_ref, *refs):
    outs = refs[len(carriers) :]
    total = keep_ref[...].astype(F32) + got_ref[...].astype(F32)
    outs[0][...] = total[:capacity].astype(BF16)
    height, units = outs[1].shape[1:]
    for k in range(1, experts):
        piece = total[k * capacity : (k + 1) * capacity]
        blank = -piece.shape[1] % units
        if blank:
            piece = jnp.concatenate([piece, jnp.zeros((capacity, blank), F32)], axis=1)
        strips = [piece[:, at : at + units] for at in range(0, piece.shape[1], units)]
        spare = height - len(strips) * capacity
        if spare:
            strips.append(jnp.zeros((spare, units), F32))
        outs[k][outs[k].shape[0] - 1] = jnp.concatenate(strips, axis=0).astype(BF16)


def combine_kernel(capacity, masks_ref, *refs):
    got, out_ref = refs[:-1], refs[-1]
    width = out_ref.shape[1]
    pieces = []
    for ref in got:
        if len(ref.shape) == 2:
            pieces.append(ref[...].astype(F32))
            continue
        block = ref[ref.shape[0] - 1].astype(F32)
        strips = [
            block[n * capacity : (n + 1) * capacity] for n in range(-(-width // block.shape[1]))
        ]
        pieces.append(jnp.concatenate(strips, axis=1)[:, :width])
    out_ref[...] = lax.dot_general(
        masks_ref[...], jnp.concatenate(pieces, axis=0).astype(BF16), (((0,), (0,)), ((), ())),
        preferred_element_type=F32,
    ).astype(BF16)


def slice_for(owner_ref, me, target, experts):
    j = 0
    for i in range(experts):
        j = jnp.where(owner_ref[me, i] == target, i, j)
    return j


def arrange_kernel(experts, groups, owner_ref, master_any, first_any, second_any, *refs):
    outs, (held, sems) = refs[: len(groups)], refs[len(groups) :]
    me = lax.axis_index("expert")
    height = held.shape[2]
    stored = (master_any, first_any, second_any)
    masters, others = [], []
    for g, (k, parts, _) in enumerate(groups):
        j = slice_for(owner_ref, me, me ^ k, experts)
        rows = pl.ds(pl.multiple_of(j * height, height), height)
        for n, i in enumerate(parts):
            target = held.at[k] if i == 0 else outs[g].at[pl.ds(3 * n, 3)]
            copy = pltpu.make_async_copy(stored[i].at[:, rows, :], target, sems.at[k, i])
            copy.start()
            if i == 0:
                masters.append((copy, k, g, n))
            else:
                others.append(copy)
    for copy, k, g, n in masters:
        copy.wait()
        for m in range(3):
            outs[g][3 * n + m] = held[k, m].astype(BF16)
    for copy in others:
        copy.wait()


def weight_kernel(experts, dp_count, with_piece, owner_ref, *refs):
    mine, other = refs[:dp_count], refs[dp_count : 2 * dp_count]
    hidden = refs[2 * dp_count : 3 * dp_count]
    packed = refs[3 * dp_count : 3 * dp_count + len(with_piece)]
    outs = refs[3 * dp_count + len(with_piece) : -3]
    rows_ref, hidden_ref, held = refs[-3:]
    me = lax.axis_index("expert")
    core = lax.axis_index("cuts")
    part = lax.axis_index("dp")
    height = outs[0].shape[1]
    units = outs[0].shape[2]
    slots = hidden[0].shape[0]
    half = mine[0].shape[2] // 2
    per_half = half // height
    for k, piece in zip(with_piece, packed):
        outs[k][3] = piece[0]
    for k in range(dp_count):
        hidden_ref[k * slots : (k + 1) * slots] = hidden[k][...]
    for source, side in ((mine, core), (other, 1 - core)):
        rows_ref[:slots] = source[0][part]
        for a in range(1, dp_count):
            rows_ref[a * slots : (a + 1) * slots] = source[a][...]
        sums = [
            lax.dot_general(
                rows_ref[:, at : at + half], hidden_ref[:, low:high], (((0,), (0,)), ((), ())),
                preferred_element_type=F32,
            )
            * (1.0 / dp_count)
            for at, low, high in (
                (0, 0, units), (0, units, 2 * units), (half, 2 * units, 3 * units),
            )
        ]
        for i in range(per_half):
            for m in range(3):
                held[m] = sums[m][i * height : (i + 1) * height].astype(BF16)
            k_of = owner_ref[me, side * per_half + i] ^ me
            for k in range(experts):

                @pl.when(k_of == k)
                def _():
                    outs[k][:3] = held[...]


def adam_kernel(k, places, grad_ref, *refs):
    outs, held, sems = refs[-7:-4], refs[-4:-1], refs[-1]
    block = lax.axis_index("expert") ^ k
    copies = []
    for m in range(3):
        master, first, second = [refs[ref][3 * n + m] for ref, n in places]
        values = adam_update(master.astype(F32), first, second, grad_ref[m].astype(F32))
        for i in range(3):
            held[i][m] = values[i].astype(held[i].dtype)
            copies.append(
                pltpu.make_async_copy(held[i].at[m], outs[i].at[block, m], sems.at[m, i])
            )
            copies[-1].start()
    for copy in copies:
        copy.wait()


def call(kernel, out_shape, n_in, smem=(), held=(), scratch=(), limit=16, flops=0, moved=0):
    specs = [
        SMEM if i in smem else HBM if i in held else VMEM
        for i in range(n_in)
    ]
    return pl.pallas_call(
        kernel,
        out_shape=out_shape,
        in_specs=specs,
        out_specs=jax.tree.map(lambda _: VMEM, out_shape),
        scratch_shapes=list(scratch),
        compiler_params=pltpu.CompilerParams(vmem_limit_bytes=limit * MIB),
        cost_estimate=pl.CostEstimate(flops=flops, bytes_accessed=moved, transcendentals=0),
    )


def shape(*dims, dtype=BF16):
    return jax.ShapeDtypeStruct(dims, dtype)


def adam_step(states, places, grad, k, buffers, experts):
    parts = 3
    height, units = grad.shape[1:]
    types = (F32, BF16, BF16)
    return pl.pallas_call(
        functools.partial(adam_kernel, k, places),
        out_shape=[shape(experts, parts, height, units, dtype=t) for t in types],
        in_specs=[VMEM] * (1 + len(states)) + [HBM] * len(buffers),
        out_specs=[HBM] * 3,
        scratch_shapes=[pltpu.VMEM((parts, height, units), t) for t in types]
        + [pltpu.SemaphoreType.DMA((parts, 3))],
        input_output_aliases={1 + len(states) + i: i for i in range(len(buffers))},
        compiler_params=pltpu.CompilerParams(vmem_limit_bytes=16 * MIB),
        cost_estimate=pl.CostEstimate(
            flops=20 * parts * height * units,
            bytes_accessed=16 * parts * height * units,
            transcendentals=2 * parts * height * units,
        ),
    )(grad, *states, *buffers)


def exchange(tensor, axis, k, count):
    return lax.ppermute(tensor, axis, [(i, i ^ k) for i in range(count)])


def after(values, *others):
    return lax.optimization_barrier((values, others))[0]


def aligned_local(
    activations,
    out_grad,
    expert_ids,
    gate_up_weight,
    down_weight,
    master_weight,
    first_moment,
    second_moment,
    new_owner,
):
    experts = lax.axis_size("expert")
    dp_count = lax.axis_size("dp")
    cores = lax.axis_size("cuts")
    row_count, model_width = activations.shape
    capacity = row_count // experts + max(1, row_count // (4 * experts))
    slots = experts * capacity
    shard_rows = model_width // dp_count
    half = shard_rows // cores
    height = shard_rows // experts
    units = master_weight.shape[3]
    ids = expert_ids.reshape(1, row_count)
    gate_up = gate_up_weight[0].reshape(model_width, 2 * units)
    down = down_weight[0]

    *sent, masks = call(
        functools.partial(dispatch_kernel, experts, capacity, dp_count),
        [shape(dp_count, capacity, 2 * half)] * experts + [shape(slots, row_count)],
        3,
        held=(0, 1, 2),
        scratch=[
            pltpu.VMEM((1, row_count), jnp.int32),
            pltpu.VMEM((2, row_count, model_width), BF16),
            pltpu.SemaphoreType.DMA((3,)),
        ],
        limit=DISPATCH_LIMIT,
        flops=2 * slots * row_count * model_width,
        moved=2 * row_count * model_width + 4 * slots * model_width,
    )(ids, activations, out_grad)
    got = [sent[0]] + [exchange(sent[k], "expert", k, experts) for k in range(1, experts)]

    near = [k for k in range(1, experts) if k.bit_count() == 1]
    far = [k for k in range(1, experts) if k.bit_count() > 1]
    early = [(k, (0, 1, 2), 0) for k in near]
    carriers = [(k, (0, 1, 2), 1) for k in far]
    groups = [(0, (0, 1, 2), 0)] + early + carriers
    stored = [t[0].transpose(1, 0, 2) for t in (master_weight, first_moment, second_moment)]
    states = call(
        functools.partial(arrange_kernel, experts, groups),
        [shape(3 * len(parts) + more, height, units) for _, parts, more in groups],
        4,
        smem=(0,),
        held=(1, 2, 3),
        scratch=[
            pltpu.VMEM((experts, 3, height, units), F32),
            pltpu.SemaphoreType.DMA((experts, 3)),
        ],
        moved=14 * shard_rows * 3 * units,
    )(new_owner, *stored)
    got, states, gate_up = lax.optimization_barrier((got, states, gate_up))
    states = dict(zip(groups, states))

    def send_states(some, *others):
        for group in some:
            states[group] = exchange(after(states[group], *others), "expert", group[0], experts)
        return [states[group] for group in some]

    sent_states = send_states(early)

    mine, *parts = call(
        functools.partial(collect_kernel, experts, dp_count),
        [shape(dp_count, slots, 2 * half)] + [shape(slots, 2 * half)] * (dp_count - 1),
        experts,
        moved=12 * slots * model_width,
    )(*got)
    other = exchange(mine, "cuts", 1, cores)

    rows = {1: exchange(parts[0], "dp", 1, dp_count)}

    hidden = call(
        functools.partial(expert_kernel, dp_count),
        shape(slots, 3 * units),
        4,
        flops=6 * slots * model_width * units,
        moved=6 * model_width * units + 8 * slots * model_width,
    )(mine, other, gate_up, down)

    keep, give = call(
        slot_grad_kernel,
        [shape(slots, model_width // cores)] * 2,
        2,
        flops=4 * slots * model_width * units,
        moved=4 * model_width * units + 4 * slots * model_width,
    )(after(hidden, rows[1]), gate_up)
    taken = exchange(give, "cuts", 1, cores)
    summed = [shape(capacity, model_width // cores)] + [shape(1, height, units)] * (experts - 1)
    for group in carriers:
        summed[group[0]] = shape(*states[group].shape)
    summed = pl.pallas_call(
        functools.partial(split_kernel, experts, capacity, far),
        out_shape=summed,
        in_specs=[VMEM] * (2 + len(far)),
        out_specs=[VMEM] * experts,
        input_output_aliases={2 + i: k for i, k in enumerate(far)},
        compiler_params=pltpu.CompilerParams(vmem_limit_bytes=16 * MIB),
        cost_estimate=pl.CostEstimate(
            flops=slots * model_width, bytes_accessed=6 * slots * model_width, transcendentals=0
        ),
    )(keep, taken, *[states[group] for group in carriers])
    for group in carriers:
        states[group] = summed[group[0]]
    send_states(carriers, sent_states)

    hiddens = {0: hidden, 2: exchange(hidden, "dp", 2, dp_count)}
    hiddens[1] = exchange(hidden, "dp", 1, dp_count)
    passed = call(pass_kernel, shape(*hidden.shape), 1, flops=PASS_FLOPS)(
        after(hiddens[2], hiddens[1], rows[1])
    )
    hiddens[3] = exchange(passed, "dp", 1, dp_count)
    for k in range(2, dp_count):
        rows[k] = exchange(parts[k - 1], "dp", k, dp_count)
    hiddens = [hiddens[k] for k in range(dp_count)]
    rows_mine = [mine] + [rows[k] for k in range(1, dp_count)]
    rows_other = [other] + [exchange(rows[k], "cuts", 1, cores) for k in range(1, dp_count)]

    grads = call(
        functools.partial(weight_kernel, experts, dp_count, near),
        [shape(3 + (k in near), height, units) for k in range(experts)],
        1 + 3 * dp_count + len(near),
        smem=(0,),
        scratch=[
            pltpu.VMEM((slots * dp_count, 2 * half), BF16),
            pltpu.VMEM((slots * dp_count, 3 * units), BF16),
            pltpu.VMEM((3, height, units), BF16),
        ],
        flops=6 * slots * dp_count * shard_rows * units,
        moved=4 * slots * dp_count * (shard_rows + units),
    )(new_owner, *rows_mine, *rows_other, *hiddens, *[summed[k] for k in near])
    moved_grads = {0: grads[0]}
    for k in near + far:
        moved_grads[k] = exchange(grads[k], "expert", k, experts)

    returned = {**moved_grads, 0: summed[0]}
    returned.update({group[0]: states[group] for group in carriers})
    input_grad = call(
        functools.partial(combine_kernel, capacity),
        shape(row_count, model_width // cores),
        1 + experts,
        flops=2 * slots * row_count * model_width // cores,
        moved=4 * slots * model_width // cores,
    )(masks, *[returned[k] for k in range(experts)])

    buffers = ()
    for k in range(experts):
        held = [group for group in groups if group[0] == k]
        places = [
            next((n, group[1].index(i)) for n, group in enumerate(held) if i in group[1])
            for i in range(3)
        ]
        buffers = adam_step(
            [states[group] for group in held], places, moved_grads[k], k, buffers, experts
        )
    outs = [b.transpose(0, 2, 1, 3)[None] for b in buffers]
    return (input_grad, *outs)


def plain_local(
    activations,
    out_grad,
    expert_ids,
    gate_up_weight,
    down_weight,
    master_weight,
    first_moment,
    second_moment,
    new_owner,
):
    experts = lax.axis_size("expert")
    dp_count = lax.axis_size("dp")
    row_count = activations.shape[0]
    model_width = activations.shape[1]
    capacity = row_count // experts + max(1, row_count // (4 * experts))
    shard_rows = model_width // dp_count
    slice_rows = shard_rows // experts
    unit_count = master_weight.shape[3]
    expert_index = lax.axis_index("expert")
    owners = lax.dynamic_slice_in_dim(new_owner, expert_index, 1, 0)[0]
    send_order = jnp.argsort(owners)
    scatter = functools.partial(
        lax.all_to_all, axis_name="expert", split_axis=0, concat_axis=0, tiled=True
    )

    def arrange(tensor):
        return jnp.take(tensor.reshape(experts, slice_rows, 3, unit_count), send_order, axis=0)

    early_master = scatter(arrange(master_weight[0]).astype(BF16)).astype(F32)
    early_first = scatter(arrange(first_moment[0]))
    early_second = scatter(arrange(second_moment[0]))
    row_expert = expert_ids[:, 0]
    onehot = (row_expert[:, None] == jnp.arange(experts, dtype=jnp.int32)[None, :]).astype(
        jnp.int32
    )
    within = jnp.sum(jnp.cumsum(onehot, axis=0) * onehot, axis=1) - 1
    target = row_expert * capacity + within
    dispatch = (
        jnp.arange(experts * capacity, dtype=jnp.int32)[:, None] == target[None, :]
    ).astype(BF16)
    rows = jnp.concatenate([activations, out_grad], axis=1)
    sent = jnp.dot(dispatch, rows, preferred_element_type=F32).astype(BF16)
    got = scatter(sent.reshape(experts, capacity, 2 * model_width))
    got = got.reshape(experts * capacity, 2 * model_width)
    slots_in, slots_grad = got[:, :model_width], got[:, model_width:]
    gate_up = gate_up_weight[0].reshape(model_width, -1)
    projected = jnp.dot(slots_in, gate_up, preferred_element_type=F32)
    hidden_grad = jnp.dot(slots_grad, down_weight[0], preferred_element_type=F32)
    gate_grad, lift_grad, hidden = expert_grads(
        projected[:, :unit_count], projected[:, unit_count:], hidden_grad
    )
    pair_grad = jnp.concatenate([gate_grad, lift_grad], axis=1)
    slot_grad = lax.dot_general(
        pair_grad, gate_up, (((1,), (1,)), ((), ())), preferred_element_type=F32
    )
    returned = scatter(slot_grad.astype(BF16).reshape(experts, capacity, model_width))
    row_grad = lax.dot_general(
        dispatch,
        returned.reshape(experts * capacity, model_width),
        (((0,), (0,)), ((), ())),
        preferred_element_type=F32,
    )
    input_grad = lax.psum_scatter(row_grad.astype(BF16), "cuts", scatter_dimension=1, tiled=True)
    paired = lax.dot_general(
        slots_in, pair_grad, (((0,), (0,)), ((), ())), preferred_element_type=F32
    )
    downed = lax.dot_general(
        slots_grad, hidden, (((0,), (0,)), ((), ())), preferred_element_type=F32
    )
    summed = lax.psum_scatter(
        jnp.concatenate([paired, downed], axis=1).astype(BF16),
        "dp",
        scatter_dimension=0,
        tiled=True,
    ).astype(F32)
    gradient = summed.reshape(shard_rows, 3, unit_count) / dp_count
    moved_gradient = scatter(arrange(gradient).astype(BF16)).astype(F32)
    moved_master, first_new, second_new = adam_update(
        early_master, early_first, early_second, moved_gradient
    )
    return (
        input_grad,
        moved_master[None],
        first_new.astype(BF16)[None],
        second_new.astype(BF16)[None],
    )


def local(*args):
    experts = lax.axis_size("expert")
    dp_count = lax.axis_size("dp")
    cores = lax.axis_size("cuts")
    row_count, model_width = args[0].shape
    capacity = row_count // experts + max(1, row_count // (4 * experts))
    height = model_width // (dp_count * experts)
    whole_tiles = (
        experts & (experts - 1) == 0
        and dp_count & (dp_count - 1) == 0
        and cores == 2
        and capacity % 8 == 0
        and (experts * capacity) % 16 == 0
        and row_count % 128 == 0
        and height % 128 == 0
        and (model_width // (dp_count * cores)) % height == 0
        and args[5].shape[3] % 128 == 0
        and -(-(model_width // cores) // args[5].shape[3]) * capacity <= height
    )
    return (aligned_local if whole_tiles else plain_local)(*args)


def solution(mesh):
    in_specs = (
        P(("expert", "dp"), None),
        P(("expert", "dp"), None),
        P(("expert", "dp"), None),
        P("expert", None, None, "cuts"),
        P("expert", None, "cuts"),
        P("expert", "dp", None, "cuts"),
        P("expert", "dp", None, "cuts"),
        P("expert", "dp", None, "cuts"),
        P(),
    )
    out_specs = (
        P(("expert", "dp"), "cuts"),
        P("expert", None, "dp", None, "cuts"),
        P("expert", None, "dp", None, "cuts"),
        P("expert", None, "dp", None, "cuts"),
    )
    return jax.shard_map(local, mesh=mesh, in_specs=in_specs, out_specs=out_specs, check_vma=False)
```

```python
import functools

import jax
import jax.numpy as jnp
from jax import lax
from jax.experimental import pallas as pl
from jax.experimental.pallas import tpu as pltpu
from jax.sharding import PartitionSpec as P

beta_first = 0.9
beta_second = 0.95
learn_rate = 0.01
decay_rate = 0.1
epsilon = 1e-08

F32 = jnp.float32
BF16 = jnp.bfloat16
VMEM = pl.BlockSpec(memory_space=pltpu.VMEM)
SMEM = pl.BlockSpec(memory_space=pltpu.SMEM)
HBM = pl.BlockSpec(memory_space=pltpu.HBM)
MIB = 1 << 20
DISPATCH_LIMIT = 60
PASS_FLOPS = 2 * 10**9


def adam_update(master, first_old, second_old, gradient):
    first_new = beta_first * first_old.astype(F32) + (1.0 - beta_first) * gradient
    second_new = beta_second * second_old.astype(F32) + (1.0 - beta_second) * gradient * gradient
    master_new = master - learn_rate * (
        first_new / (jnp.sqrt(second_new) + epsilon) + decay_rate * master
    )
    return (master_new, first_new, second_new)


def expert_grads(gate, lift, hidden_grad):
    sigmoid = jax.nn.sigmoid(gate)
    silu = gate * sigmoid
    hidden = (silu * lift).astype(BF16)
    lift_grad = (hidden_grad * silu).astype(BF16)
    gate_grad = (hidden_grad * lift * sigmoid * (1.0 + gate * (1.0 - sigmoid))).astype(BF16)
    return gate_grad, lift_grad, hidden


def slot_masks(ids, me, experts, capacity):
    rows = ids.shape[1]
    high = max(8, experts)
    match = lax.broadcasted_iota(jnp.int32, (high, rows), 0) == ids
    onehot = jnp.where(match, 1.0, 0.0)
    earlier = jnp.where(
        lax.broadcasted_iota(jnp.int32, (rows, rows), 0)
        < lax.broadcasted_iota(jnp.int32, (rows, rows), 1),
        1.0,
        0.0,
    )
    counts = jnp.dot(onehot.astype(BF16), earlier.astype(BF16), preferred_element_type=F32)
    within = jnp.sum(onehot * counts, axis=0, keepdims=True).astype(jnp.int32)
    slot = lax.broadcasted_iota(jnp.int32, (capacity, rows), 0)
    masks = [
        jnp.where(jnp.where(ids == (me ^ k), within, -1) == slot, 1.0, 0.0) for k in range(experts)
    ]
    return jnp.concatenate(masks, axis=0).astype(BF16)


def dispatch_kernel(experts, capacity, dp_count, ids_any, in_any, grad_any, *refs):
    outs, (masks_ref, ids_ref, held, sems) = refs[:experts], refs[experts:]
    me = lax.axis_index("expert")
    core = lax.axis_index("cuts")
    half = outs[0].shape[2] // 2
    cores = in_any.shape[1] // (dp_count * half)
    first = pltpu.make_async_copy(ids_any, ids_ref, sems.at[2])
    first.start()
    copies = [
        pltpu.make_async_copy(x_any, held.at[x], sems.at[x])
        for x, x_any in enumerate((in_any, grad_any))
    ]
    for copy in copies:
        copy.start()
    first.wait()
    masks = slot_masks(ids_ref[...], me, experts, capacity)
    masks_ref[...] = masks
    for x in range(2):
        copies[x].wait()
        for q in range(dp_count):
            columns = pl.ds(pl.multiple_of((q * cores + core) * half, half), half)
            picked = jnp.dot(masks, held[x, :, columns], preferred_element_type=F32)
            for k in range(experts):
                outs[k][q, :, x * half : (x + 1) * half] = picked[
                    k * capacity : (k + 1) * capacity
                ].astype(BF16)


def collect_kernel(experts, dp_count, *refs):
    got, whole, parts = refs[:experts], refs[experts], refs[experts + 1 :]
    part = lax.axis_index("dp")
    for q in range(dp_count):
        joined = jnp.concatenate([got[k][q].astype(F32) for k in range(experts)], axis=0)
        whole[q] = joined.astype(BF16)
    for k in range(1, dp_count):
        parts[k - 1][...] = whole[part ^ k]


def expert_kernel(dp_count, mine_ref, other_ref, gate_up_ref, down_ref, out_ref):
    core = lax.axis_index("cuts")
    half = mine_ref.shape[2] // 2
    units = down_ref.shape[1]
    rows = mine_ref.shape[1]
    projected = jnp.zeros((rows, 2 * units), F32)
    hidden_grad = jnp.zeros((rows, units), F32)
    for x_ref, side in ((mine_ref, core), (other_ref, 1 - core)):
        for q in range(dp_count):
            depth = pl.ds(pl.multiple_of((2 * q + side) * half, half), half)
            projected += jnp.dot(x_ref[q, :, :half], gate_up_ref[depth, :], preferred_element_type=F32)
            hidden_grad += jnp.dot(x_ref[q, :, half:], down_ref[depth, :], preferred_element_type=F32)
    gate_grad, lift_grad, hidden = expert_grads(
        projected[:, :units], projected[:, units:], hidden_grad
    )
    out_ref[:, :units] = gate_grad
    out_ref[:, units : 2 * units] = lift_grad
    out_ref[:, 2 * units :] = hidden


def pass_kernel(got_ref, out_ref):
    out_ref[...] = got_ref[...]


def slot_grad_kernel(pair_ref, gate_up_ref, keep_ref, send_ref):
    core = lax.axis_index("cuts")
    width = keep_ref.shape[1]
    units = gate_up_ref.shape[1]
    pair = pair_ref[:, :units]
    for out_ref, side in ((keep_ref, core), (send_ref, 1 - core)):
        depth = pl.ds(pl.multiple_of(side * width, width), width)
        out_ref[...] = lax.dot_general(
            pair, gate_up_ref[depth, :], (((1,), (1,)), ((), ())), preferred_element_type=F32
        ).astype(BF16)


def split_kernel(experts, capacity, carriers, keep_ref, got_ref, *refs):
    outs = refs[len(carriers) :]
    total = keep_ref[...].astype(F32) + got_ref[...].astype(F32)
    outs[0][...] = total[:capacity].astype(BF16)
    height, units = outs[1].shape[1:]
    for k in range(1, experts):
        piece = total[k * capacity : (k + 1) * capacity]
        blank = -piece.shape[1] % units
        if blank:
            piece = jnp.concatenate([piece, jnp.zeros((capacity, blank), F32)], axis=1)
        strips = [piece[:, at : at + units] for at in range(0, piece.shape[1], units)]
        spare = height - len(strips) * capacity
        if spare:
            strips.append(jnp.zeros((spare, units), F32))
        outs[k][outs[k].shape[0] - 1] = jnp.concatenate(strips, axis=0).astype(BF16)


def combine_kernel(capacity, masks_ref, *refs):
    got, out_ref = refs[:-1], refs[-1]
    width = out_ref.shape[1]
    pieces = []
    for ref in got:
        if len(ref.shape) == 2:
            pieces.append(ref[...].astype(F32))
            continue
        block = ref[ref.shape[0] - 1].astype(F32)
        strips = [
            block[n * capacity : (n + 1) * capacity] for n in range(-(-width // block.shape[1]))
        ]
        pieces.append(jnp.concatenate(strips, axis=1)[:, :width])
    out_ref[...] = lax.dot_general(
        masks_ref[...], jnp.concatenate(pieces, axis=0).astype(BF16), (((0,), (0,)), ((), ())),
        preferred_element_type=F32,
    ).astype(BF16)


def slice_for(owner_ref, me, target, experts):
    j = 0
    for i in range(experts):
        j = jnp.where(owner_ref[me, i] == target, i, j)
    return j


def arrange_kernel(experts, groups, owner_ref, master_any, first_any, second_any, *refs):
    outs, (held, sems) = refs[: len(groups)], refs[len(groups) :]
    me = lax.axis_index("expert")
    height = held.shape[2]
    stored = (master_any, first_any, second_any)
    masters, others = [], []
    for g, (k, parts, _) in enumerate(groups):
        j = slice_for(owner_ref, me, me ^ k, experts)
        rows = pl.ds(pl.multiple_of(j * height, height), height)
        for n, i in enumerate(parts):
            target = held.at[k] if i == 0 else outs[g].at[pl.ds(3 * n, 3)]
            copy = pltpu.make_async_copy(stored[i].at[:, rows, :], target, sems.at[k, i])
            copy.start()
            if i == 0:
                masters.append((copy, k, g, n))
            else:
                others.append(copy)
    for copy, k, g, n in masters:
        copy.wait()
        for m in range(3):
            outs[g][3 * n + m] = held[k, m].astype(BF16)
    for copy in others:
        copy.wait()


def weight_kernel(experts, dp_count, ks, with_piece, owner_ref, *refs):
    mine, other = refs[:dp_count], refs[dp_count : 2 * dp_count]
    hidden = refs[2 * dp_count : 3 * dp_count]
    packed = refs[3 * dp_count : 3 * dp_count + len(with_piece)]
    outs = refs[3 * dp_count + len(with_piece) : -2]
    rows_ref, hidden_ref = refs[-2:]
    me = lax.axis_index("expert")
    core = lax.axis_index("cuts")
    part = lax.axis_index("dp")
    height, units = outs[0].shape[1:]
    slots = hidden[0].shape[0]
    half = mine[0].shape[2] // 2
    per_half = half // height
    for n in range(dp_count):
        place = slice(n * slots, (n + 1) * slots)
        hidden_ref[place] = hidden[n][...]
        for side, source in enumerate((mine, other)):
            rows_ref[side, place] = source[0][part] if n == 0 else source[n][...]
    for out, k in zip(outs, ks):
        j = slice_for(owner_ref, me, me ^ k, experts)
        side = jnp.where(j // per_half == core, 0, 1)
        at = lax.rem(j, per_half) * height
        for m, offset in enumerate((0, 0, half)):
            columns = pl.ds(pl.multiple_of(at + offset, height), height)
            total = lax.dot_general(
                rows_ref[side, :, columns],
                hidden_ref[:, m * units : (m + 1) * units],
                (((0,), (0,)), ((), ())),
                preferred_element_type=F32,
            )
            out[m] = (total * (1.0 / dp_count)).astype(BF16)
        if k in with_piece:
            out[3] = packed[with_piece.index(k)][0]


def adam_kernel(tasks, *refs):
    outs, held, sems = refs[-7:-4], refs[-4:-1], refs[-1]
    me = lax.axis_index("expert")
    copies, at = [], 0
    for t, (k, places) in enumerate(tasks):
        grad_ref, states = refs[at], refs[at + 1 :]
        at += 2 + max(ref for ref, _ in places)
        for m in range(3):
            master, first, second = [states[ref][3 * n + m] for ref, n in places]
            values = adam_update(master.astype(F32), first, second, grad_ref[m].astype(F32))
            for i in range(3):
                held[i][t, m] = values[i].astype(held[i].dtype)
                copies.append(
                    pltpu.make_async_copy(
                        held[i].at[t, m], outs[i].at[me ^ k, m], sems.at[t, m, i]
                    )
                )
                copies[-1].start()
    for copy in copies:
        copy.wait()


def call(kernel, out_shape, n_in, smem=(), held=(), scratch=(), limit=16, flops=0, moved=0):
    specs = [
        SMEM if i in smem else HBM if i in held else VMEM
        for i in range(n_in)
    ]
    return pl.pallas_call(
        kernel,
        out_shape=out_shape,
        in_specs=specs,
        out_specs=jax.tree.map(lambda _: VMEM, out_shape),
        scratch_shapes=list(scratch),
        compiler_params=pltpu.CompilerParams(vmem_limit_bytes=limit * MIB),
        cost_estimate=pl.CostEstimate(flops=flops, bytes_accessed=moved, transcendentals=0),
    )


def shape(*dims, dtype=BF16):
    return jax.ShapeDtypeStruct(dims, dtype)


def adam_step(tasks, buffers, experts):
    parts = 3
    height, units = tasks[0][2].shape[1:]
    types = (F32, BF16, BF16)
    inputs = [t for _, _, grad, states in tasks for t in (grad, *states)]
    size = len(tasks) * parts * height * units
    return pl.pallas_call(
        functools.partial(adam_kernel, [(k, places) for k, places, _, _ in tasks]),
        out_shape=[shape(experts, parts, height, units, dtype=t) for t in types],
        in_specs=[VMEM] * len(inputs) + [HBM] * len(buffers),
        out_specs=[HBM] * 3,
        scratch_shapes=[pltpu.VMEM((len(tasks), parts, height, units), t) for t in types]
        + [pltpu.SemaphoreType.DMA((len(tasks), parts, 3))],
        input_output_aliases={len(inputs) + i: i for i in range(len(buffers))},
        compiler_params=pltpu.CompilerParams(vmem_limit_bytes=16 * MIB),
        cost_estimate=pl.CostEstimate(
            flops=20 * size, bytes_accessed=16 * size, transcendentals=2 * size
        ),
    )(*inputs, *buffers)


def exchange(tensor, axis, k, count):
    return lax.ppermute(tensor, axis, [(i, i ^ k) for i in range(count)])


def after(values, *others):
    return lax.optimization_barrier((values, others))[0]


def aligned_local(
    activations,
    out_grad,
    expert_ids,
    gate_up_weight,
    down_weight,
    master_weight,
    first_moment,
    second_moment,
    new_owner,
):
    experts = lax.axis_size("expert")
    dp_count = lax.axis_size("dp")
    cores = lax.axis_size("cuts")
    row_count, model_width = activations.shape
    capacity = row_count // experts + max(1, row_count // (4 * experts))
    slots = experts * capacity
    shard_rows = model_width // dp_count
    half = shard_rows // cores
    height = shard_rows // experts
    units = master_weight.shape[3]
    ids = expert_ids.reshape(1, row_count)
    gate_up = gate_up_weight[0].reshape(model_width, 2 * units)
    down = down_weight[0]

    *sent, masks = call(
        functools.partial(dispatch_kernel, experts, capacity, dp_count),
        [shape(dp_count, capacity, 2 * half)] * experts + [shape(slots, row_count)],
        3,
        held=(0, 1, 2),
        scratch=[
            pltpu.VMEM((1, row_count), jnp.int32),
            pltpu.VMEM((2, row_count, model_width), BF16),
            pltpu.SemaphoreType.DMA((3,)),
        ],
        limit=DISPATCH_LIMIT,
        flops=2 * slots * row_count * model_width,
        moved=2 * row_count * model_width + 4 * slots * model_width,
    )(ids, activations, out_grad)
    got = [sent[0]] + [exchange(sent[k], "expert", k, experts) for k in range(1, experts)]

    near = [k for k in range(1, experts) if k.bit_count() == 1]
    far = [k for k in range(1, experts) if k.bit_count() > 1]
    early = [(k, (0, 1, 2), 0) for k in far]
    carriers = [(k, (0, 1, 2), 1) for k in near]
    groups = [(0, (0, 1, 2), 0)] + early + carriers
    stored = [t[0].transpose(1, 0, 2) for t in (master_weight, first_moment, second_moment)]
    states = call(
        functools.partial(arrange_kernel, experts, groups),
        [shape(3 * len(parts) + more, height, units) for _, parts, more in groups],
        4,
        smem=(0,),
        held=(1, 2, 3),
        scratch=[
            pltpu.VMEM((experts, 3, height, units), F32),
            pltpu.SemaphoreType.DMA((experts, 3)),
        ],
        moved=14 * shard_rows * 3 * units,
    )(new_owner, *stored)
    got, states, gate_up = lax.optimization_barrier((got, states, gate_up))
    states = dict(zip(groups, states))

    def send_states(some, *others):
        for group in some:
            states[group] = exchange(after(states[group], *others), "expert", group[0], experts)
        return [states[group] for group in some]

    sent_states = send_states(early)

    mine, *parts = call(
        functools.partial(collect_kernel, experts, dp_count),
        [shape(dp_count, slots, 2 * half)] + [shape(slots, 2 * half)] * (dp_count - 1),
        experts,
        moved=12 * slots * model_width,
    )(*got)
    other = exchange(mine, "cuts", 1, cores)

    rows = {1: exchange(parts[0], "dp", 1, dp_count)}

    hidden = call(
        functools.partial(expert_kernel, dp_count),
        shape(slots, 3 * units),
        4,
        flops=6 * slots * model_width * units,
        moved=6 * model_width * units + 8 * slots * model_width,
    )(mine, other, gate_up, down)

    keep, give = call(
        slot_grad_kernel,
        [shape(slots, model_width // cores)] * 2,
        2,
        flops=4 * slots * model_width * units,
        moved=4 * model_width * units + 4 * slots * model_width,
    )(after(hidden, rows[1]), gate_up)
    taken = exchange(give, "cuts", 1, cores)
    summed = [shape(capacity, model_width // cores)] + [shape(1, height, units)] * (experts - 1)
    for group in carriers:
        summed[group[0]] = shape(*states[group].shape)
    summed = pl.pallas_call(
        functools.partial(split_kernel, experts, capacity, near),
        out_shape=summed,
        in_specs=[VMEM] * (2 + len(near)),
        out_specs=[VMEM] * experts,
        input_output_aliases={2 + i: k for i, k in enumerate(near)},
        compiler_params=pltpu.CompilerParams(vmem_limit_bytes=16 * MIB),
        cost_estimate=pl.CostEstimate(
            flops=slots * model_width, bytes_accessed=6 * slots * model_width, transcendentals=0
        ),
    )(keep, taken, *[states[group] for group in carriers])
    summed = list(summed)
    for group in carriers:
        states[group] = summed[group[0]]

    hiddens = {0: hidden, 2: exchange(hidden, "dp", 2, dp_count)}
    hiddens[1] = exchange(hidden, "dp", 1, dp_count)
    send_states(carriers, sent_states)
    passed = call(pass_kernel, shape(*hidden.shape), 1, flops=PASS_FLOPS)(
        after(hiddens[2], hiddens[1], rows[1])
    )
    hiddens[3] = exchange(passed, "dp", 1, dp_count)
    rows[3] = exchange(parts[2], "dp", 3, dp_count)
    rows[2] = exchange(after(parts[1], rows[3]), "dp", 2, dp_count)
    hiddens = [hiddens[k] for k in range(dp_count)]
    rows_mine = [mine] + [rows[k] for k in range(1, dp_count)]
    rows_other = [other] + [exchange(rows[k], "cuts", 1, cores) for k in range(1, dp_count)]

    grads = {}
    for ks in (near, far + [0]):
        some = [k for k in ks if k in far]
        made = call(
            functools.partial(weight_kernel, experts, dp_count, ks, some),
            [shape(3 + (k in some), height, units) for k in ks],
            1 + 3 * dp_count + len(some),
            smem=(0,),
            scratch=[
                pltpu.VMEM((2, slots * dp_count, 2 * half), BF16),
                pltpu.VMEM((slots * dp_count, 3 * units), BF16),
            ],
            flops=6 * slots * dp_count * height * len(ks) * units,
            moved=4 * slots * dp_count * (shard_rows + units),
        )(new_owner, *rows_mine, *rows_other, *hiddens, *[summed[k] for k in some])
        grads.update(zip(ks, made))
    moved_grads = {0: grads[0]}
    for k in near + far:
        moved_grads[k] = exchange(grads[k], "expert", k, experts)

    returned = {**moved_grads, 0: summed[0]}
    returned.update({group[0]: states[group] for group in carriers})
    input_grad = call(
        functools.partial(combine_kernel, capacity),
        shape(row_count, model_width // cores),
        1 + experts,
        flops=2 * slots * row_count * model_width // cores,
        moved=4 * slots * model_width // cores,
    )(masks, *[returned[k] for k in range(experts)])

    buffers = ()
    for ks in ([0], far, near):
        tasks = []
        for k in ks:
            held = [group for group in groups if group[0] == k]
            places = [
                next((n, group[1].index(i)) for n, group in enumerate(held) if i in group[1])
                for i in range(3)
            ]
            tasks.append((k, places, moved_grads[k], [states[group] for group in held]))
        buffers = adam_step(tasks, buffers, experts)
    outs = [b.transpose(0, 2, 1, 3)[None] for b in buffers]
    return (input_grad, *outs)


def plain_local(
    activations,
    out_grad,
    expert_ids,
    gate_up_weight,
    down_weight,
    master_weight,
    first_moment,
    second_moment,
    new_owner,
):
    experts = lax.axis_size("expert")
    dp_count = lax.axis_size("dp")
    row_count = activations.shape[0]
    model_width = activations.shape[1]
    capacity = row_count // experts + max(1, row_count // (4 * experts))
    shard_rows = model_width // dp_count
    slice_rows = shard_rows // experts
    unit_count = master_weight.shape[3]
    expert_index = lax.axis_index("expert")
    owners = lax.dynamic_slice_in_dim(new_owner, expert_index, 1, 0)[0]
    send_order = jnp.argsort(owners)
    scatter = functools.partial(
        lax.all_to_all, axis_name="expert", split_axis=0, concat_axis=0, tiled=True
    )

    def arrange(tensor):
        return jnp.take(tensor.reshape(experts, slice_rows, 3, unit_count), send_order, axis=0)

    early_master = scatter(arrange(master_weight[0]).astype(BF16)).astype(F32)
    early_first = scatter(arrange(first_moment[0]))
    early_second = scatter(arrange(second_moment[0]))
    row_expert = expert_ids[:, 0]
    onehot = (row_expert[:, None] == jnp.arange(experts, dtype=jnp.int32)[None, :]).astype(
        jnp.int32
    )
    within = jnp.sum(jnp.cumsum(onehot, axis=0) * onehot, axis=1) - 1
    target = row_expert * capacity + within
    dispatch = (
        jnp.arange(experts * capacity, dtype=jnp.int32)[:, None] == target[None, :]
    ).astype(BF16)
    rows = jnp.concatenate([activations, out_grad], axis=1)
    sent = jnp.dot(dispatch, rows, preferred_element_type=F32).astype(BF16)
    got = scatter(sent.reshape(experts, capacity, 2 * model_width))
    got = got.reshape(experts * capacity, 2 * model_width)
    slots_in, slots_grad = got[:, :model_width], got[:, model_width:]
    gate_up = gate_up_weight[0].reshape(model_width, -1)
    projected = jnp.dot(slots_in, gate_up, preferred_element_type=F32)
    hidden_grad = jnp.dot(slots_grad, down_weight[0], preferred_element_type=F32)
    gate_grad, lift_grad, hidden = expert_grads(
        projected[:, :unit_count], projected[:, unit_count:], hidden_grad
    )
    pair_grad = jnp.concatenate([gate_grad, lift_grad], axis=1)
    slot_grad = lax.dot_general(
        pair_grad, gate_up, (((1,), (1,)), ((), ())), preferred_element_type=F32
    )
    returned = scatter(slot_grad.astype(BF16).reshape(experts, capacity, model_width))
    row_grad = lax.dot_general(
        dispatch,
        returned.reshape(experts * capacity, model_width),
        (((0,), (0,)), ((), ())),
        preferred_element_type=F32,
    )
    input_grad = lax.psum_scatter(row_grad.astype(BF16), "cuts", scatter_dimension=1, tiled=True)
    paired = lax.dot_general(
        slots_in, pair_grad, (((0,), (0,)), ((), ())), preferred_element_type=F32
    )
    downed = lax.dot_general(
        slots_grad, hidden, (((0,), (0,)), ((), ())), preferred_element_type=F32
    )
    summed = lax.psum_scatter(
        jnp.concatenate([paired, downed], axis=1).astype(BF16),
        "dp",
        scatter_dimension=0,
        tiled=True,
    ).astype(F32)
    gradient = summed.reshape(shard_rows, 3, unit_count) / dp_count
    moved_gradient = scatter(arrange(gradient).astype(BF16)).astype(F32)
    moved_master, first_new, second_new = adam_update(
        early_master, early_first, early_second, moved_gradient
    )
    return (
        input_grad,
        moved_master[None],
        first_new.astype(BF16)[None],
        second_new.astype(BF16)[None],
    )


def local(*args):
    experts = lax.axis_size("expert")
    dp_count = lax.axis_size("dp")
    cores = lax.axis_size("cuts")
    row_count, model_width = args[0].shape
    capacity = row_count // experts + max(1, row_count // (4 * experts))
    height = model_width // (dp_count * experts)
    whole_tiles = (
        experts & (experts - 1) == 0
        and experts >= 4
        and dp_count == 4
        and cores == 2
        and capacity % 8 == 0
        and (experts * capacity) % 16 == 0
        and row_count % 128 == 0
        and height % 128 == 0
        and (model_width // (dp_count * cores)) % height == 0
        and args[5].shape[3] % 128 == 0
        and -(-(model_width // cores) // args[5].shape[3]) * capacity <= height
    )
    return (aligned_local if whole_tiles else plain_local)(*args)


def solution(mesh):
    in_specs = (
        P(("expert", "dp"), None),
        P(("expert", "dp"), None),
        P(("expert", "dp"), None),
        P("expert", None, None, "cuts"),
        P("expert", None, "cuts"),
        P("expert", "dp", None, "cuts"),
        P("expert", "dp", None, "cuts"),
        P("expert", "dp", None, "cuts"),
        P(),
    )
    out_specs = (
        P(("expert", "dp"), "cuts"),
        P("expert", None, "dp", None, "cuts"),
        P("expert", None, "dp", None, "cuts"),
        P("expert", None, "dp", None, "cuts"),
    )
    return jax.shard_map(local, mesh=mesh, in_specs=in_specs, out_specs=out_specs, check_vma=False)
```

```python
import functools

import jax
import jax.numpy as jnp
from jax import lax
from jax.experimental import pallas as pl
from jax.experimental.pallas import tpu as pltpu
from jax.sharding import PartitionSpec as P

beta_first = 0.9
beta_second = 0.95
learn_rate = 0.01
decay_rate = 0.1
epsilon = 1e-08

F32 = jnp.float32
BF16 = jnp.bfloat16
VMEM = pl.BlockSpec(memory_space=pltpu.VMEM)
SMEM = pl.BlockSpec(memory_space=pltpu.SMEM)
HBM = pl.BlockSpec(memory_space=pltpu.HBM)
MIB = 1 << 20
DISPATCH_LIMIT = 60
PASS_FLOPS = 2 * 10**9


def adam_update(master, first_old, second_old, gradient):
    first_new = beta_first * first_old.astype(F32) + (1.0 - beta_first) * gradient
    second_new = beta_second * second_old.astype(F32) + (1.0 - beta_second) * gradient * gradient
    master_new = master - learn_rate * (
        first_new / (jnp.sqrt(second_new) + epsilon) + decay_rate * master
    )
    return (master_new, first_new, second_new)


def expert_grads(gate, lift, hidden_grad):
    sigmoid = jax.nn.sigmoid(gate)
    silu = gate * sigmoid
    hidden = (silu * lift).astype(BF16)
    lift_grad = (hidden_grad * silu).astype(BF16)
    gate_grad = (hidden_grad * lift * sigmoid * (1.0 + gate * (1.0 - sigmoid))).astype(BF16)
    return gate_grad, lift_grad, hidden


def slot_masks(ids, me, experts, capacity):
    rows = ids.shape[1]
    high = max(8, experts)
    match = lax.broadcasted_iota(jnp.int32, (high, rows), 0) == ids
    onehot = jnp.where(match, 1.0, 0.0)
    earlier = jnp.where(
        lax.broadcasted_iota(jnp.int32, (rows, rows), 0)
        < lax.broadcasted_iota(jnp.int32, (rows, rows), 1),
        1.0,
        0.0,
    )
    counts = jnp.dot(onehot.astype(BF16), earlier.astype(BF16), preferred_element_type=F32)
    within = jnp.sum(onehot * counts, axis=0, keepdims=True).astype(jnp.int32)
    slot = lax.broadcasted_iota(jnp.int32, (capacity, rows), 0)
    masks = [
        jnp.where(jnp.where(ids == (me ^ k), within, -1) == slot, 1.0, 0.0) for k in range(experts)
    ]
    return jnp.concatenate(masks, axis=0).astype(BF16)


def dispatch_kernel(experts, capacity, dp_count, ids_any, in_any, grad_any, *refs):
    outs, (masks_ref, ids_ref, held, sems) = refs[:experts], refs[experts:]
    me = lax.axis_index("expert")
    core = lax.axis_index("cuts")
    half = outs[0].shape[2] // 2
    cores = in_any.shape[1] // (dp_count * half)
    first = pltpu.make_async_copy(ids_any, ids_ref, sems.at[2])
    first.start()
    copies = [
        pltpu.make_async_copy(x_any, held.at[x], sems.at[x])
        for x, x_any in enumerate((in_any, grad_any))
    ]
    for copy in copies:
        copy.start()
    first.wait()
    masks = slot_masks(ids_ref[...], me, experts, capacity)
    masks_ref[...] = masks
    for x in range(2):
        copies[x].wait()
        for q in range(dp_count):
            columns = pl.ds(pl.multiple_of((q * cores + core) * half, half), half)
            picked = jnp.dot(masks, held[x, :, columns], preferred_element_type=F32)
            for k in range(experts):
                outs[k][q, :, x * half : (x + 1) * half] = picked[
                    k * capacity : (k + 1) * capacity
                ].astype(BF16)


def collect_kernel(experts, dp_count, *refs):
    got, whole, parts = refs[:experts][::-1], refs[experts], refs[experts + 1 :]
    part = lax.axis_index("dp")
    for q in range(dp_count):
        joined = jnp.concatenate([got[k][q].astype(F32) for k in range(experts)], axis=0)
        whole[q] = joined.astype(BF16)
    for k in range(1, dp_count):
        parts[k - 1][...] = whole[part ^ k]


def expert_kernel(dp_count, mine_ref, other_ref, gate_up_ref, down_ref, out_ref):
    core = lax.axis_index("cuts")
    half = mine_ref.shape[2] // 2
    units = down_ref.shape[1]
    rows = mine_ref.shape[1]
    projected = jnp.zeros((rows, 2 * units), F32)
    hidden_grad = jnp.zeros((rows, units), F32)
    for x_ref, side in ((mine_ref, core), (other_ref, 1 - core)):
        for q in range(dp_count):
            depth = pl.ds(pl.multiple_of((2 * q + side) * half, half), half)
            projected += jnp.dot(x_ref[q, :, :half], gate_up_ref[depth, :], preferred_element_type=F32)
            hidden_grad += jnp.dot(x_ref[q, :, half:], down_ref[depth, :], preferred_element_type=F32)
    gate_grad, lift_grad, hidden = expert_grads(
        projected[:, :units], projected[:, units:], hidden_grad
    )
    out_ref[:, :units] = gate_grad
    out_ref[:, units : 2 * units] = lift_grad
    out_ref[:, 2 * units :] = hidden


def pass_kernel(got_ref, out_ref):
    out_ref[...] = got_ref[...]


def slot_grad_kernel(pair_ref, gate_up_ref, keep_ref, send_ref):
    core = lax.axis_index("cuts")
    width = keep_ref.shape[1]
    units = gate_up_ref.shape[1]
    pair = pair_ref[:, :units]
    for out_ref, side in ((keep_ref, core), (send_ref, 1 - core)):
        depth = pl.ds(pl.multiple_of(side * width, width), width)
        out_ref[...] = lax.dot_general(
            pair, gate_up_ref[depth, :], (((1,), (1,)), ((), ())), preferred_element_type=F32
        ).astype(BF16)


def split_kernel(experts, capacity, carriers, keep_ref, got_ref, *refs):
    outs = refs[len(carriers) :]
    total = keep_ref[...].astype(F32) + got_ref[...].astype(F32)
    outs[0][...] = total[:capacity].astype(BF16)
    height, units = outs[1].shape[1:]
    for k in range(1, experts):
        piece = total[k * capacity : (k + 1) * capacity]
        blank = -piece.shape[1] % units
        if blank:
            piece = jnp.concatenate([piece, jnp.zeros((capacity, blank), F32)], axis=1)
        strips = [piece[:, at : at + units] for at in range(0, piece.shape[1], units)]
        spare = height - len(strips) * capacity
        if spare:
            strips.append(jnp.zeros((spare, units), F32))
        outs[k][outs[k].shape[0] - 1] = jnp.concatenate(strips, axis=0).astype(BF16)


def combine_kernel(capacity, masks_ref, *refs):
    got, out_ref = refs[:-1], refs[-1]
    width = out_ref.shape[1]
    pieces = []
    for ref in got:
        if len(ref.shape) == 2:
            pieces.append(ref[...].astype(F32))
            continue
        block = ref[ref.shape[0] - 1].astype(F32)
        strips = [
            block[n * capacity : (n + 1) * capacity] for n in range(-(-width // block.shape[1]))
        ]
        pieces.append(jnp.concatenate(strips, axis=1)[:, :width])
    out_ref[...] = lax.dot_general(
        masks_ref[...], jnp.concatenate(pieces, axis=0).astype(BF16), (((0,), (0,)), ((), ())),
        preferred_element_type=F32,
    ).astype(BF16)


def slice_for(owner_ref, me, target, experts):
    j = 0
    for i in range(experts):
        j = jnp.where(owner_ref[me, i] == target, i, j)
    return j


def arrange_kernel(experts, groups, owner_ref, master_any, first_any, second_any, *refs):
    outs, (held, sems) = refs[: len(groups)], refs[len(groups) :]
    me = lax.axis_index("expert")
    height = held.shape[2]
    stored = (master_any, first_any, second_any)
    masters, others = [], []
    for g, (k, parts, _) in enumerate(groups):
        j = slice_for(owner_ref, me, me ^ k, experts)
        rows = pl.ds(pl.multiple_of(j * height, height), height)
        for n, i in enumerate(parts):
            target = held.at[k] if i == 0 else outs[g].at[pl.ds(3 * n, 3)]
            copy = pltpu.make_async_copy(stored[i].at[:, rows, :], target, sems.at[k, i])
            copy.start()
            if i == 0:
                masters.append((copy, k, g, n))
            else:
                others.append(copy)
    for copy, k, g, n in masters:
        copy.wait()
        for m in range(3):
            outs[g][3 * n + m] = held[k, m].astype(BF16)
    for copy in others:
        copy.wait()


def weight_kernel(experts, dp_count, ks, with_piece, owner_ref, *refs):
    mine, other = refs[:dp_count], refs[dp_count : 2 * dp_count]
    hidden = refs[2 * dp_count : 3 * dp_count]
    packed = refs[3 * dp_count : 3 * dp_count + len(with_piece)]
    outs = refs[3 * dp_count + len(with_piece) : -2]
    rows_ref, hidden_ref = refs[-2:]
    me = lax.axis_index("expert")
    core = lax.axis_index("cuts")
    part = lax.axis_index("dp")
    height, units = outs[0].shape[1:]
    slots = hidden[0].shape[0]
    half = mine[0].shape[2] // 2
    per_half = half // height
    for n in range(dp_count):
        place = slice(n * slots, (n + 1) * slots)
        hidden_ref[place] = hidden[n][...]
        for side, source in enumerate((mine, other)):
            rows_ref[side, place] = source[0][part] if n == 0 else source[n][...]
    for out, k in zip(outs, ks):
        j = slice_for(owner_ref, me, me ^ k, experts)
        side = jnp.where(j // per_half == core, 0, 1)
        at = lax.rem(j, per_half) * height
        for m, offset in enumerate((0, 0, half)):
            columns = pl.ds(pl.multiple_of(at + offset, height), height)
            total = lax.dot_general(
                rows_ref[side, :, columns],
                hidden_ref[:, m * units : (m + 1) * units],
                (((0,), (0,)), ((), ())),
                preferred_element_type=F32,
            )
            out[m] = (total * (1.0 / dp_count)).astype(BF16)
        if k in with_piece:
            out[3] = packed[with_piece.index(k)][0]


def adam_kernel(tasks, *refs):
    outs, held, sems = refs[-7:-4], refs[-4:-1], refs[-1]
    me = lax.axis_index("expert")
    copies, at = [], 0
    for t, (k, places) in enumerate(tasks):
        grad_ref, states = refs[at], refs[at + 1 :]
        at += 2 + max(ref for ref, _ in places)
        for m in range(3):
            master, first, second = [states[ref][3 * n + m] for ref, n in places]
            values = adam_update(master.astype(F32), first, second, grad_ref[m].astype(F32))
            for i in range(3):
                held[i][t, m] = values[i].astype(held[i].dtype)
                copies.append(
                    pltpu.make_async_copy(
                        held[i].at[t, m], outs[i].at[me ^ k, m], sems.at[t, m, i]
                    )
                )
                copies[-1].start()
    for copy in copies:
        copy.wait()


def call(kernel, out_shape, n_in, smem=(), held=(), scratch=(), limit=16, flops=0, moved=0):
    specs = [
        SMEM if i in smem else HBM if i in held else VMEM
        for i in range(n_in)
    ]
    return pl.pallas_call(
        kernel,
        out_shape=out_shape,
        in_specs=specs,
        out_specs=jax.tree.map(lambda _: VMEM, out_shape),
        scratch_shapes=list(scratch),
        compiler_params=pltpu.CompilerParams(vmem_limit_bytes=limit * MIB),
        cost_estimate=pl.CostEstimate(flops=flops, bytes_accessed=moved, transcendentals=0),
    )


def shape(*dims, dtype=BF16):
    return jax.ShapeDtypeStruct(dims, dtype)


def adam_step(tasks, buffers, experts):
    parts = 3
    height, units = tasks[0][2].shape[1:]
    types = (F32, BF16, BF16)
    inputs = [t for _, _, grad, states in tasks for t in (grad, *states)]
    size = len(tasks) * parts * height * units
    return pl.pallas_call(
        functools.partial(adam_kernel, [(k, places) for k, places, _, _ in tasks]),
        out_shape=[shape(experts, parts, height, units, dtype=t) for t in types],
        in_specs=[VMEM] * len(inputs) + [HBM] * len(buffers),
        out_specs=[HBM] * 3,
        scratch_shapes=[pltpu.VMEM((len(tasks), parts, height, units), t) for t in types]
        + [pltpu.SemaphoreType.DMA((len(tasks), parts, 3))],
        input_output_aliases={len(inputs) + i: i for i in range(len(buffers))},
        compiler_params=pltpu.CompilerParams(vmem_limit_bytes=16 * MIB),
        cost_estimate=pl.CostEstimate(
            flops=20 * size, bytes_accessed=16 * size, transcendentals=2 * size
        ),
    )(*inputs, *buffers)


def exchange(tensor, axis, k, count):
    return lax.ppermute(tensor, axis, [(i, i ^ k) for i in range(count)])


def after(values, *others):
    return lax.optimization_barrier((values, others))[0]


def aligned_local(
    activations,
    out_grad,
    expert_ids,
    gate_up_weight,
    down_weight,
    master_weight,
    first_moment,
    second_moment,
    new_owner,
):
    experts = lax.axis_size("expert")
    dp_count = lax.axis_size("dp")
    cores = lax.axis_size("cuts")
    row_count, model_width = activations.shape
    capacity = row_count // experts + max(1, row_count // (4 * experts))
    slots = experts * capacity
    shard_rows = model_width // dp_count
    half = shard_rows // cores
    height = shard_rows // experts
    units = master_weight.shape[3]
    ids = expert_ids.reshape(1, row_count)
    gate_up = gate_up_weight[0].reshape(model_width, 2 * units)
    down = down_weight[0]

    *sent, masks = call(
        functools.partial(dispatch_kernel, experts, capacity, dp_count),
        [shape(dp_count, capacity, 2 * half)] * experts + [shape(slots, row_count)],
        3,
        held=(0, 1, 2),
        scratch=[
            pltpu.VMEM((1, row_count), jnp.int32),
            pltpu.VMEM((2, row_count, model_width), BF16),
            pltpu.SemaphoreType.DMA((3,)),
        ],
        limit=DISPATCH_LIMIT,
        flops=2 * slots * row_count * model_width,
        moved=2 * row_count * model_width + 4 * slots * model_width,
    )(ids, activations, out_grad)
    got = [sent[0]] + [exchange(sent[k], "expert", k, experts) for k in range(1, experts)]

    near = [k for k in range(1, experts) if k.bit_count() == 1]
    far = [k for k in range(1, experts) if k.bit_count() > 1]
    early = [(k, (0, 1, 2), 0) for k in far]
    carriers = [(k, (0, 1, 2), 1) for k in near]
    groups = [(0, (0, 1, 2), 0)] + early + carriers
    stored = [t[0].transpose(1, 0, 2) for t in (master_weight, first_moment, second_moment)]
    states = call(
        functools.partial(arrange_kernel, experts, groups),
        [shape(3 * len(parts) + more, height, units) for _, parts, more in groups],
        4,
        smem=(0,),
        held=(1, 2, 3),
        scratch=[
            pltpu.VMEM((experts, 3, height, units), F32),
            pltpu.SemaphoreType.DMA((experts, 3)),
        ],
        moved=14 * shard_rows * 3 * units,
    )(new_owner, *stored)
    got, states, gate_up = lax.optimization_barrier((got[::-1], states, gate_up))
    states = dict(zip(groups, states))

    def send_states(some, *others):
        for group in some:
            states[group] = exchange(after(states[group], *others), "expert", group[0], experts)
        return [states[group] for group in some]

    sent_states = send_states(early)

    mine, *parts = call(
        functools.partial(collect_kernel, experts, dp_count),
        [shape(dp_count, slots, 2 * half)] + [shape(slots, 2 * half)] * (dp_count - 1),
        experts,
        moved=12 * slots * model_width,
    )(*got)
    other = exchange(mine, "cuts", 1, cores)

    rows = {1: exchange(parts[0], "dp", 1, dp_count)}

    hidden = call(
        functools.partial(expert_kernel, dp_count),
        shape(slots, 3 * units),
        4,
        flops=6 * slots * model_width * units,
        moved=6 * model_width * units + 8 * slots * model_width,
    )(mine, other, gate_up, down)

    keep, give = call(
        slot_grad_kernel,
        [shape(slots, model_width // cores)] * 2,
        2,
        flops=4 * slots * model_width * units,
        moved=4 * model_width * units + 4 * slots * model_width,
    )(after(hidden, rows[1]), gate_up)
    taken = exchange(give, "cuts", 1, cores)
    summed = [shape(capacity, model_width // cores)] + [shape(1, height, units)] * (experts - 1)
    for group in carriers:
        summed[group[0]] = shape(*states[group].shape)
    summed = pl.pallas_call(
        functools.partial(split_kernel, experts, capacity, near),
        out_shape=summed,
        in_specs=[VMEM] * (2 + len(near)),
        out_specs=[VMEM] * experts,
        input_output_aliases={2 + i: k for i, k in enumerate(near)},
        compiler_params=pltpu.CompilerParams(vmem_limit_bytes=16 * MIB),
        cost_estimate=pl.CostEstimate(
            flops=slots * model_width, bytes_accessed=6 * slots * model_width, transcendentals=0
        ),
    )(keep, taken, *[states[group] for group in carriers])
    summed = list(summed)
    for group in carriers:
        states[group] = summed[group[0]]

    hiddens = {0: hidden, 2: exchange(hidden, "dp", 2, dp_count)}
    hiddens[1] = exchange(hidden, "dp", 1, dp_count)
    send_states(carriers[:1])
    send_states(carriers[1:], sent_states)
    passed = call(pass_kernel, shape(*hidden.shape), 1, flops=PASS_FLOPS)(
        after(hiddens[2], hiddens[1], rows[1])
    )
    hiddens[3] = exchange(passed, "dp", 1, dp_count)
    rows[3] = exchange(parts[2], "dp", 3, dp_count)
    rows[2] = exchange(after(parts[1], rows[3]), "dp", 2, dp_count)
    hiddens = [hiddens[k] for k in range(dp_count)]
    rows_mine = [mine] + [rows[k] for k in range(1, dp_count)]
    rows_other = [other] + [exchange(rows[k], "cuts", 1, cores) for k in range(1, dp_count)]

    grads = {}
    for ks in (near, far + [0]):
        some = [k for k in ks if k in far]
        made = call(
            functools.partial(weight_kernel, experts, dp_count, ks, some),
            [shape(3 + (k in some), height, units) for k in ks],
            1 + 3 * dp_count + len(some),
            smem=(0,),
            scratch=[
                pltpu.VMEM((2, slots * dp_count, 2 * half), BF16),
                pltpu.VMEM((slots * dp_count, 3 * units), BF16),
            ],
            flops=6 * slots * dp_count * height * len(ks) * units,
            moved=4 * slots * dp_count * (shard_rows + units),
        )(new_owner, *rows_mine, *rows_other, *hiddens, *[summed[k] for k in some])
        grads.update(zip(ks, made))
    moved_grads = {0: grads[0]}
    for k in near + far:
        moved_grads[k] = exchange(grads[k], "expert", k, experts)

    returned = {**moved_grads, 0: summed[0]}
    returned.update({group[0]: states[group] for group in carriers})
    input_grad = call(
        functools.partial(combine_kernel, capacity),
        shape(row_count, model_width // cores),
        1 + experts,
        flops=2 * slots * row_count * model_width // cores,
        moved=4 * slots * model_width // cores,
    )(masks, *[returned[k] for k in range(experts)])

    buffers = ()
    for ks in ([0], far, near):
        tasks = []
        for k in ks:
            held = [group for group in groups if group[0] == k]
            places = [
                next((n, group[1].index(i)) for n, group in enumerate(held) if i in group[1])
                for i in range(3)
            ]
            tasks.append((k, places, moved_grads[k], [states[group] for group in held]))
        buffers = adam_step(tasks, buffers, experts)
    outs = [b.transpose(0, 2, 1, 3)[None] for b in buffers]
    return (input_grad, *outs)


def plain_local(
    activations,
    out_grad,
    expert_ids,
    gate_up_weight,
    down_weight,
    master_weight,
    first_moment,
    second_moment,
    new_owner,
):
    experts = lax.axis_size("expert")
    dp_count = lax.axis_size("dp")
    row_count = activations.shape[0]
    model_width = activations.shape[1]
    capacity = row_count // experts + max(1, row_count // (4 * experts))
    shard_rows = model_width // dp_count
    slice_rows = shard_rows // experts
    unit_count = master_weight.shape[3]
    expert_index = lax.axis_index("expert")
    owners = lax.dynamic_slice_in_dim(new_owner, expert_index, 1, 0)[0]
    send_order = jnp.argsort(owners)
    scatter = functools.partial(
        lax.all_to_all, axis_name="expert", split_axis=0, concat_axis=0, tiled=True
    )

    def arrange(tensor):
        return jnp.take(tensor.reshape(experts, slice_rows, 3, unit_count), send_order, axis=0)

    early_master = scatter(arrange(master_weight[0]).astype(BF16)).astype(F32)
    early_first = scatter(arrange(first_moment[0]))
    early_second = scatter(arrange(second_moment[0]))
    row_expert = expert_ids[:, 0]
    onehot = (row_expert[:, None] == jnp.arange(experts, dtype=jnp.int32)[None, :]).astype(
        jnp.int32
    )
    within = jnp.sum(jnp.cumsum(onehot, axis=0) * onehot, axis=1) - 1
    target = row_expert * capacity + within
    dispatch = (
        jnp.arange(experts * capacity, dtype=jnp.int32)[:, None] == target[None, :]
    ).astype(BF16)
    rows = jnp.concatenate([activations, out_grad], axis=1)
    sent = jnp.dot(dispatch, rows, preferred_element_type=F32).astype(BF16)
    got = scatter(sent.reshape(experts, capacity, 2 * model_width))
    got = got.reshape(experts * capacity, 2 * model_width)
    slots_in, slots_grad = got[:, :model_width], got[:, model_width:]
    gate_up = gate_up_weight[0].reshape(model_width, -1)
    projected = jnp.dot(slots_in, gate_up, preferred_element_type=F32)
    hidden_grad = jnp.dot(slots_grad, down_weight[0], preferred_element_type=F32)
    gate_grad, lift_grad, hidden = expert_grads(
        projected[:, :unit_count], projected[:, unit_count:], hidden_grad
    )
    pair_grad = jnp.concatenate([gate_grad, lift_grad], axis=1)
    slot_grad = lax.dot_general(
        pair_grad, gate_up, (((1,), (1,)), ((), ())), preferred_element_type=F32
    )
    returned = scatter(slot_grad.astype(BF16).reshape(experts, capacity, model_width))
    row_grad = lax.dot_general(
        dispatch,
        returned.reshape(experts * capacity, model_width),
        (((0,), (0,)), ((), ())),
        preferred_element_type=F32,
    )
    input_grad = lax.psum_scatter(row_grad.astype(BF16), "cuts", scatter_dimension=1, tiled=True)
    paired = lax.dot_general(
        slots_in, pair_grad, (((0,), (0,)), ((), ())), preferred_element_type=F32
    )
    downed = lax.dot_general(
        slots_grad, hidden, (((0,), (0,)), ((), ())), preferred_element_type=F32
    )
    summed = lax.psum_scatter(
        jnp.concatenate([paired, downed], axis=1).astype(BF16),
        "dp",
        scatter_dimension=0,
        tiled=True,
    ).astype(F32)
    gradient = summed.reshape(shard_rows, 3, unit_count) / dp_count
    moved_gradient = scatter(arrange(gradient).astype(BF16)).astype(F32)
    moved_master, first_new, second_new = adam_update(
        early_master, early_first, early_second, moved_gradient
    )
    return (
        input_grad,
        moved_master[None],
        first_new.astype(BF16)[None],
        second_new.astype(BF16)[None],
    )


def local(*args):
    experts = lax.axis_size("expert")
    dp_count = lax.axis_size("dp")
    cores = lax.axis_size("cuts")
    row_count, model_width = args[0].shape
    capacity = row_count // experts + max(1, row_count // (4 * experts))
    height = model_width // (dp_count * experts)
    whole_tiles = (
        experts & (experts - 1) == 0
        and experts >= 4
        and dp_count == 4
        and cores == 2
        and capacity % 8 == 0
        and (experts * capacity) % 16 == 0
        and row_count % 128 == 0
        and height % 128 == 0
        and (model_width // (dp_count * cores)) % height == 0
        and args[5].shape[3] % 128 == 0
        and -(-(model_width // cores) // args[5].shape[3]) * capacity <= height
    )
    return (aligned_local if whole_tiles else plain_local)(*args)


def solution(mesh):
    in_specs = (
        P(("expert", "dp"), None),
        P(("expert", "dp"), None),
        P(("expert", "dp"), None),
        P("expert", None, None, "cuts"),
        P("expert", None, "cuts"),
        P("expert", "dp", None, "cuts"),
        P("expert", "dp", None, "cuts"),
        P("expert", "dp", None, "cuts"),
        P(),
    )
    out_specs = (
        P(("expert", "dp"), "cuts"),
        P("expert", None, "dp", None, "cuts"),
        P("expert", None, "dp", None, "cuts"),
        P("expert", None, "dp", None, "cuts"),
    )
    return jax.shard_map(local, mesh=mesh, in_specs=in_specs, out_specs=out_specs, check_vma=False)
```

```python
import functools

import jax
import jax.numpy as jnp
from jax import lax
from jax.experimental import pallas as pl
from jax.experimental.pallas import tpu as pltpu
from jax.sharding import PartitionSpec as P

beta_first = 0.9
beta_second = 0.95
learn_rate = 0.01
decay_rate = 0.1
epsilon = 1e-08

F32 = jnp.float32
BF16 = jnp.bfloat16
VMEM = pl.BlockSpec(memory_space=pltpu.VMEM)
SMEM = pl.BlockSpec(memory_space=pltpu.SMEM)
HBM = pl.BlockSpec(memory_space=pltpu.HBM)
MIB = 1 << 20
DISPATCH_LIMIT = 60
PASS_FLOPS = 2 * 10**9


def adam_update(master, first_old, second_old, gradient):
    first_new = beta_first * first_old.astype(F32) + (1.0 - beta_first) * gradient
    second_new = beta_second * second_old.astype(F32) + (1.0 - beta_second) * gradient * gradient
    master_new = master - learn_rate * (
        first_new / (jnp.sqrt(second_new) + epsilon) + decay_rate * master
    )
    return (master_new, first_new, second_new)


def expert_grads(gate, lift, hidden_grad):
    sigmoid = jax.nn.sigmoid(gate)
    silu = gate * sigmoid
    hidden = (silu * lift).astype(BF16)
    lift_grad = (hidden_grad * silu).astype(BF16)
    gate_grad = (hidden_grad * lift * sigmoid * (1.0 + gate * (1.0 - sigmoid))).astype(BF16)
    return gate_grad, lift_grad, hidden


def slot_masks(ids, me, experts, capacity):
    rows = ids.shape[1]
    high = max(8, experts)
    match = lax.broadcasted_iota(jnp.int32, (high, rows), 0) == ids
    onehot = jnp.where(match, 1.0, 0.0)
    earlier = jnp.where(
        lax.broadcasted_iota(jnp.int32, (rows, rows), 0)
        < lax.broadcasted_iota(jnp.int32, (rows, rows), 1),
        1.0,
        0.0,
    )
    counts = jnp.dot(onehot.astype(BF16), earlier.astype(BF16), preferred_element_type=F32)
    within = jnp.sum(onehot * counts, axis=0, keepdims=True).astype(jnp.int32)
    slot = lax.broadcasted_iota(jnp.int32, (capacity, rows), 0)
    masks = [
        jnp.where(jnp.where(ids == (me ^ k), within, -1) == slot, 1.0, 0.0) for k in range(experts)
    ]
    return jnp.concatenate(masks, axis=0).astype(BF16)


def dispatch_kernel(experts, capacity, dp_count, ids_any, in_any, grad_any, *refs):
    outs, (masks_ref, ids_ref, held, sems) = refs[:experts], refs[experts:]
    me = lax.axis_index("expert")
    core = lax.axis_index("cuts")
    half = outs[0].shape[2] // 2
    cores = in_any.shape[1] // (dp_count * half)
    first = pltpu.make_async_copy(ids_any, ids_ref, sems.at[2])
    first.start()
    copies = [
        pltpu.make_async_copy(x_any, held.at[x], sems.at[x])
        for x, x_any in enumerate((in_any, grad_any))
    ]
    for copy in copies:
        copy.start()
    first.wait()
    masks = slot_masks(ids_ref[...], me, experts, capacity)
    masks_ref[...] = masks
    for x in range(2):
        copies[x].wait()
        for q in range(dp_count):
            columns = pl.ds(pl.multiple_of((q * cores + core) * half, half), half)
            picked = jnp.dot(masks, held[x, :, columns], preferred_element_type=F32)
            for k in range(experts):
                outs[k][q, :, x * half : (x + 1) * half] = picked[
                    k * capacity : (k + 1) * capacity
                ].astype(BF16)


def collect_kernel(experts, dp_count, *refs):
    got, whole, parts = refs[:experts][::-1], refs[experts], refs[experts + 1 :]
    part = lax.axis_index("dp")
    for q in range(dp_count):
        joined = jnp.concatenate([got[k][q].astype(F32) for k in range(experts)], axis=0)
        whole[q] = joined.astype(BF16)
    for k in range(1, dp_count):
        parts[k - 1][...] = whole[part ^ k]


def expert_kernel(dp_count, mine_ref, other_ref, gate_up_ref, down_ref, out_ref):
    core = lax.axis_index("cuts")
    half = mine_ref.shape[2] // 2
    units = down_ref.shape[1]
    rows = mine_ref.shape[1]
    projected = jnp.zeros((rows, 2 * units), F32)
    hidden_grad = jnp.zeros((rows, units), F32)
    for x_ref, side in ((mine_ref, core), (other_ref, 1 - core)):
        for q in range(dp_count):
            depth = pl.ds(pl.multiple_of((2 * q + side) * half, half), half)
            projected += jnp.dot(x_ref[q, :, :half], gate_up_ref[depth, :], preferred_element_type=F32)
            hidden_grad += jnp.dot(x_ref[q, :, half:], down_ref[depth, :], preferred_element_type=F32)
    gate_grad, lift_grad, hidden = expert_grads(
        projected[:, :units], projected[:, units:], hidden_grad
    )
    out_ref[:, :units] = gate_grad
    out_ref[:, units : 2 * units] = lift_grad
    out_ref[:, 2 * units :] = hidden


def pass_kernel(got_ref, out_ref):
    out_ref[...] = got_ref[...]


def slot_grad_kernel(pair_ref, gate_up_ref, keep_ref, send_ref):
    core = lax.axis_index("cuts")
    width = keep_ref.shape[1]
    units = gate_up_ref.shape[1]
    pair = pair_ref[:, :units]
    for out_ref, side in ((keep_ref, core), (send_ref, 1 - core)):
        depth = pl.ds(pl.multiple_of(side * width, width), width)
        out_ref[...] = lax.dot_general(
            pair, gate_up_ref[depth, :], (((1,), (1,)), ((), ())), preferred_element_type=F32
        ).astype(BF16)


def split_kernel(experts, capacity, carriers, keep_ref, got_ref, *refs):
    outs = refs[len(carriers) :]
    total = keep_ref[...].astype(F32) + got_ref[...].astype(F32)
    outs[0][...] = total[:capacity].astype(BF16)
    height, units = outs[1].shape[1:]
    for k in range(1, experts):
        piece = total[k * capacity : (k + 1) * capacity]
        blank = -piece.shape[1] % units
        if blank:
            piece = jnp.concatenate([piece, jnp.zeros((capacity, blank), F32)], axis=1)
        strips = [piece[:, at : at + units] for at in range(0, piece.shape[1], units)]
        spare = height - len(strips) * capacity
        if spare:
            strips.append(jnp.zeros((spare, units), F32))
        outs[k][outs[k].shape[0] - 1] = jnp.concatenate(strips, axis=0).astype(BF16)


def combine_kernel(capacity, masks_ref, *refs):
    got, out_ref = refs[:-1], refs[-1]
    width = out_ref.shape[1]
    pieces = []
    for ref in got:
        if len(ref.shape) == 2:
            pieces.append(ref[...].astype(F32))
            continue
        block = ref[ref.shape[0] - 1].astype(F32)
        strips = [
            block[n * capacity : (n + 1) * capacity] for n in range(-(-width // block.shape[1]))
        ]
        pieces.append(jnp.concatenate(strips, axis=1)[:, :width])
    out_ref[...] = lax.dot_general(
        masks_ref[...], jnp.concatenate(pieces, axis=0).astype(BF16), (((0,), (0,)), ((), ())),
        preferred_element_type=F32,
    ).astype(BF16)


def slice_for(owner_ref, me, target, experts):
    j = 0
    for i in range(experts):
        j = jnp.where(owner_ref[me, i] == target, i, j)
    return j


def arrange_kernel(experts, groups, owner_ref, master_any, first_any, second_any, *refs):
    outs, (held, sems) = refs[: len(groups)], refs[len(groups) :]
    me = lax.axis_index("expert")
    height = held.shape[2]
    stored = (master_any, first_any, second_any)
    masters, others = [], []
    for g, (k, parts, _) in enumerate(groups):
        j = slice_for(owner_ref, me, me ^ k, experts)
        rows = pl.ds(pl.multiple_of(j * height, height), height)
        for n, i in enumerate(parts):
            target = held.at[k] if i == 0 else outs[g].at[pl.ds(3 * n, 3)]
            copy = pltpu.make_async_copy(stored[i].at[:, rows, :], target, sems.at[k, i])
            copy.start()
            if i == 0:
                masters.append((copy, k, g, n))
            else:
                others.append(copy)
    for copy, k, g, n in masters:
        copy.wait()
        for m in range(3):
            outs[g][3 * n + m] = held[k, m].astype(BF16)
    for copy in others:
        copy.wait()


def weight_kernel(experts, dp_count, ks, with_piece, owner_ref, *refs):
    mine, other = refs[:dp_count], refs[dp_count : 2 * dp_count]
    hidden = refs[2 * dp_count : 3 * dp_count]
    packed = refs[3 * dp_count : 3 * dp_count + len(with_piece)]
    outs = refs[3 * dp_count + len(with_piece) :]
    me = lax.axis_index("expert")
    core = lax.axis_index("cuts")
    part = lax.axis_index("dp")
    height, units = outs[0].shape[1:]
    half = mine[0].shape[2] // 2
    per_half = half // height
    factors = [
        jnp.concatenate([ref[:, m * units : (m + 1) * units] for ref in hidden], axis=0)
        for m in range(3)
    ]
    for out, k in zip(outs, ks):
        j = slice_for(owner_ref, me, me ^ k, experts)
        own_side = j // per_half == core
        at = lax.rem(j, per_half) * height
        rows = {}
        for offset in (0, half):
            columns = pl.ds(pl.multiple_of(at + offset, height), height)
            blocks = []
            for n in range(dp_count):
                place = (part, slice(None), columns) if n == 0 else (slice(None), columns)
                blocks.append(jnp.where(own_side, mine[n][place], other[n][place]))
            rows[offset] = jnp.concatenate(blocks, axis=0)
        for m, offset in enumerate((0, 0, half)):
            total = lax.dot_general(
                rows[offset], factors[m], (((0,), (0,)), ((), ())), preferred_element_type=F32
            )
            out[m] = (total * (1.0 / dp_count)).astype(BF16)
        if k in with_piece:
            out[3] = packed[with_piece.index(k)][0]


def adam_kernel(tasks, *refs):
    outs, held, sems = refs[-7:-4], refs[-4:-1], refs[-1]
    me = lax.axis_index("expert")
    copies, at = [], 0
    for t, (k, places) in enumerate(tasks):
        grad_ref, states = refs[at], refs[at + 1 :]
        at += 2 + max(ref for ref, _ in places)
        for m in range(3):
            master, first, second = [states[ref][3 * n + m] for ref, n in places]
            values = adam_update(master.astype(F32), first, second, grad_ref[m].astype(F32))
            for i in range(3):
                held[i][t, m] = values[i].astype(held[i].dtype)
                copies.append(
                    pltpu.make_async_copy(
                        held[i].at[t, m], outs[i].at[me ^ k, m], sems.at[t, m, i]
                    )
                )
                copies[-1].start()
    for copy in copies:
        copy.wait()


def call(kernel, out_shape, n_in, smem=(), held=(), scratch=(), limit=16, flops=0, moved=0):
    specs = [
        SMEM if i in smem else HBM if i in held else VMEM
        for i in range(n_in)
    ]
    return pl.pallas_call(
        kernel,
        out_shape=out_shape,
        in_specs=specs,
        out_specs=jax.tree.map(lambda _: VMEM, out_shape),
        scratch_shapes=list(scratch),
        compiler_params=pltpu.CompilerParams(vmem_limit_bytes=limit * MIB),
        cost_estimate=pl.CostEstimate(flops=flops, bytes_accessed=moved, transcendentals=0),
    )


def shape(*dims, dtype=BF16):
    return jax.ShapeDtypeStruct(dims, dtype)


def adam_step(tasks, buffers, experts):
    parts = 3
    height, units = tasks[0][2].shape[1:]
    types = (F32, BF16, BF16)
    inputs = [t for _, _, grad, states in tasks for t in (grad, *states)]
    size = len(tasks) * parts * height * units
    return pl.pallas_call(
        functools.partial(adam_kernel, [(k, places) for k, places, _, _ in tasks]),
        out_shape=[shape(experts, parts, height, units, dtype=t) for t in types],
        in_specs=[VMEM] * len(inputs) + [HBM] * len(buffers),
        out_specs=[HBM] * 3,
        scratch_shapes=[pltpu.VMEM((len(tasks), parts, height, units), t) for t in types]
        + [pltpu.SemaphoreType.DMA((len(tasks), parts, 3))],
        input_output_aliases={len(inputs) + i: i for i in range(len(buffers))},
        compiler_params=pltpu.CompilerParams(vmem_limit_bytes=16 * MIB),
        cost_estimate=pl.CostEstimate(
            flops=20 * size, bytes_accessed=16 * size, transcendentals=2 * size
        ),
    )(*inputs, *buffers)


def exchange(tensor, axis, k, count):
    return lax.ppermute(tensor, axis, [(i, i ^ k) for i in range(count)])


def after(values, *others):
    return lax.optimization_barrier((values, others))[0]


def aligned_local(
    activations,
    out_grad,
    expert_ids,
    gate_up_weight,
    down_weight,
    master_weight,
    first_moment,
    second_moment,
    new_owner,
):
    experts = lax.axis_size("expert")
    dp_count = lax.axis_size("dp")
    cores = lax.axis_size("cuts")
    row_count, model_width = activations.shape
    capacity = row_count // experts + max(1, row_count // (4 * experts))
    slots = experts * capacity
    shard_rows = model_width // dp_count
    half = shard_rows // cores
    height = shard_rows // experts
    units = master_weight.shape[3]
    ids = expert_ids.reshape(1, row_count)
    gate_up = gate_up_weight[0].reshape(model_width, 2 * units)
    down = down_weight[0]

    *sent, masks = call(
        functools.partial(dispatch_kernel, experts, capacity, dp_count),
        [shape(dp_count, capacity, 2 * half)] * experts + [shape(slots, row_count)],
        3,
        held=(0, 1, 2),
        scratch=[
            pltpu.VMEM((1, row_count), jnp.int32),
            pltpu.VMEM((2, row_count, model_width), BF16),
            pltpu.SemaphoreType.DMA((3,)),
        ],
        limit=DISPATCH_LIMIT,
        flops=2 * slots * row_count * model_width,
        moved=2 * row_count * model_width + 4 * slots * model_width,
    )(ids, activations, out_grad)
    got = [sent[0]] + [exchange(sent[k], "expert", k, experts) for k in range(1, experts)]

    near = [k for k in range(1, experts) if k.bit_count() == 1]
    far = [k for k in range(1, experts) if k.bit_count() > 1]
    early = [(k, (0, 1, 2), 0) for k in far]
    carriers = [(k, (0, 1, 2), 1) for k in near]
    groups = [(0, (0, 1, 2), 0)] + early + carriers
    stored = [t[0].transpose(1, 0, 2) for t in (master_weight, first_moment, second_moment)]
    states = call(
        functools.partial(arrange_kernel, experts, groups),
        [shape(3 * len(parts) + more, height, units) for _, parts, more in groups],
        4,
        smem=(0,),
        held=(1, 2, 3),
        scratch=[
            pltpu.VMEM((experts, 3, height, units), F32),
            pltpu.SemaphoreType.DMA((experts, 3)),
        ],
        moved=14 * shard_rows * 3 * units,
    )(new_owner, *stored)
    got, states, gate_up = lax.optimization_barrier((got[::-1], states, gate_up))
    states = dict(zip(groups, states))

    def send_states(some, *others):
        for group in some:
            states[group] = exchange(after(states[group], *others), "expert", group[0], experts)
        return [states[group] for group in some]

    sent_states = send_states(early)

    mine, *parts = call(
        functools.partial(collect_kernel, experts, dp_count),
        [shape(dp_count, slots, 2 * half)] + [shape(slots, 2 * half)] * (dp_count - 1),
        experts,
        moved=12 * slots * model_width,
    )(*got)
    other = exchange(mine, "cuts", 1, cores)

    rows = {1: exchange(parts[0], "dp", 1, dp_count)}

    hidden = call(
        functools.partial(expert_kernel, dp_count),
        shape(slots, 3 * units),
        4,
        flops=6 * slots * model_width * units,
        moved=6 * model_width * units + 8 * slots * model_width,
    )(mine, other, gate_up, down)

    keep, give = call(
        slot_grad_kernel,
        [shape(slots, model_width // cores)] * 2,
        2,
        flops=4 * slots * model_width * units,
        moved=4 * model_width * units + 4 * slots * model_width,
    )(after(hidden, rows[1]), gate_up)
    taken = exchange(give, "cuts", 1, cores)
    summed = [shape(capacity, model_width // cores)] + [shape(1, height, units)] * (experts - 1)
    for group in carriers:
        summed[group[0]] = shape(*states[group].shape)
    summed = pl.pallas_call(
        functools.partial(split_kernel, experts, capacity, near),
        out_shape=summed,
        in_specs=[VMEM] * (2 + len(near)),
        out_specs=[VMEM] * experts,
        input_output_aliases={2 + i: k for i, k in enumerate(near)},
        compiler_params=pltpu.CompilerParams(vmem_limit_bytes=16 * MIB),
        cost_estimate=pl.CostEstimate(
            flops=slots * model_width, bytes_accessed=6 * slots * model_width, transcendentals=0
        ),
    )(keep, taken, *[states[group] for group in carriers])
    summed = list(summed)
    for group in carriers:
        states[group] = summed[group[0]]

    hiddens = {0: hidden, 2: exchange(hidden, "dp", 2, dp_count)}
    hiddens[1] = exchange(hidden, "dp", 1, dp_count)
    send_states(carriers[:1])
    send_states(carriers[1:], sent_states)
    passed = call(pass_kernel, shape(*hidden.shape), 1, flops=PASS_FLOPS)(
        after(hiddens[2], hiddens[1], rows[1])
    )
    hiddens[3] = exchange(passed, "dp", 1, dp_count)
    rows[3] = exchange(parts[2], "dp", 3, dp_count)
    rows[2] = exchange(after(parts[1], rows[3]), "dp", 2, dp_count)
    hiddens = [hiddens[k] for k in range(dp_count)]
    rows_mine = [mine] + [rows[k] for k in range(1, dp_count)]
    rows_other = [other] + [exchange(rows[k], "cuts", 1, cores) for k in range(1, dp_count)]

    grads = {}
    for ks in (near, far + [0]):
        some = [k for k in ks if k in far]
        made = call(
            functools.partial(weight_kernel, experts, dp_count, ks, some),
            [shape(3 + (k in some), height, units) for k in ks],
            1 + 3 * dp_count + len(some),
            smem=(0,),
            flops=6 * slots * dp_count * height * len(ks) * units,
            moved=4 * slots * dp_count * (shard_rows + units),
        )(new_owner, *rows_mine, *rows_other, *hiddens, *[summed[k] for k in some])
        grads.update(zip(ks, made))
    moved_grads = {0: grads[0]}
    for k in near + far:
        moved_grads[k] = exchange(grads[k], "expert", k, experts)

    returned = {**moved_grads, 0: summed[0]}
    returned.update({group[0]: states[group] for group in carriers})
    input_grad = call(
        functools.partial(combine_kernel, capacity),
        shape(row_count, model_width // cores),
        1 + experts,
        flops=2 * slots * row_count * model_width // cores,
        moved=4 * slots * model_width // cores,
    )(masks, *[returned[k] for k in range(experts)])

    buffers = ()
    for ks in ([0], far, near):
        tasks = []
        for k in ks:
            held = [group for group in groups if group[0] == k]
            places = [
                next((n, group[1].index(i)) for n, group in enumerate(held) if i in group[1])
                for i in range(3)
            ]
            tasks.append((k, places, moved_grads[k], [states[group] for group in held]))
        buffers = adam_step(tasks, buffers, experts)
    outs = [b.transpose(0, 2, 1, 3)[None] for b in buffers]
    return (input_grad, *outs)


def plain_local(
    activations,
    out_grad,
    expert_ids,
    gate_up_weight,
    down_weight,
    master_weight,
    first_moment,
    second_moment,
    new_owner,
):
    experts = lax.axis_size("expert")
    dp_count = lax.axis_size("dp")
    row_count = activations.shape[0]
    model_width = activations.shape[1]
    capacity = row_count // experts + max(1, row_count // (4 * experts))
    shard_rows = model_width // dp_count
    slice_rows = shard_rows // experts
    unit_count = master_weight.shape[3]
    expert_index = lax.axis_index("expert")
    owners = lax.dynamic_slice_in_dim(new_owner, expert_index, 1, 0)[0]
    send_order = jnp.argsort(owners)
    scatter = functools.partial(
        lax.all_to_all, axis_name="expert", split_axis=0, concat_axis=0, tiled=True
    )

    def arrange(tensor):
        return jnp.take(tensor.reshape(experts, slice_rows, 3, unit_count), send_order, axis=0)

    early_master = scatter(arrange(master_weight[0]).astype(BF16)).astype(F32)
    early_first = scatter(arrange(first_moment[0]))
    early_second = scatter(arrange(second_moment[0]))
    row_expert = expert_ids[:, 0]
    onehot = (row_expert[:, None] == jnp.arange(experts, dtype=jnp.int32)[None, :]).astype(
        jnp.int32
    )
    within = jnp.sum(jnp.cumsum(onehot, axis=0) * onehot, axis=1) - 1
    target = row_expert * capacity + within
    dispatch = (
        jnp.arange(experts * capacity, dtype=jnp.int32)[:, None] == target[None, :]
    ).astype(BF16)
    rows = jnp.concatenate([activations, out_grad], axis=1)
    sent = jnp.dot(dispatch, rows, preferred_element_type=F32).astype(BF16)
    got = scatter(sent.reshape(experts, capacity, 2 * model_width))
    got = got.reshape(experts * capacity, 2 * model_width)
    slots_in, slots_grad = got[:, :model_width], got[:, model_width:]
    gate_up = gate_up_weight[0].reshape(model_width, -1)
    projected = jnp.dot(slots_in, gate_up, preferred_element_type=F32)
    hidden_grad = jnp.dot(slots_grad, down_weight[0], preferred_element_type=F32)
    gate_grad, lift_grad, hidden = expert_grads(
        projected[:, :unit_count], projected[:, unit_count:], hidden_grad
    )
    pair_grad = jnp.concatenate([gate_grad, lift_grad], axis=1)
    slot_grad = lax.dot_general(
        pair_grad, gate_up, (((1,), (1,)), ((), ())), preferred_element_type=F32
    )
    returned = scatter(slot_grad.astype(BF16).reshape(experts, capacity, model_width))
    row_grad = lax.dot_general(
        dispatch,
        returned.reshape(experts * capacity, model_width),
        (((0,), (0,)), ((), ())),
        preferred_element_type=F32,
    )
    input_grad = lax.psum_scatter(row_grad.astype(BF16), "cuts", scatter_dimension=1, tiled=True)
    paired = lax.dot_general(
        slots_in, pair_grad, (((0,), (0,)), ((), ())), preferred_element_type=F32
    )
    downed = lax.dot_general(
        slots_grad, hidden, (((0,), (0,)), ((), ())), preferred_element_type=F32
    )
    summed = lax.psum_scatter(
        jnp.concatenate([paired, downed], axis=1).astype(BF16),
        "dp",
        scatter_dimension=0,
        tiled=True,
    ).astype(F32)
    gradient = summed.reshape(shard_rows, 3, unit_count) / dp_count
    moved_gradient = scatter(arrange(gradient).astype(BF16)).astype(F32)
    moved_master, first_new, second_new = adam_update(
        early_master, early_first, early_second, moved_gradient
    )
    return (
        input_grad,
        moved_master[None],
        first_new.astype(BF16)[None],
        second_new.astype(BF16)[None],
    )


def local(*args):
    experts = lax.axis_size("expert")
    dp_count = lax.axis_size("dp")
    cores = lax.axis_size("cuts")
    row_count, model_width = args[0].shape
    capacity = row_count // experts + max(1, row_count // (4 * experts))
    height = model_width // (dp_count * experts)
    whole_tiles = (
        experts & (experts - 1) == 0
        and experts >= 4
        and dp_count == 4
        and cores == 2
        and capacity % 8 == 0
        and (experts * capacity) % 16 == 0
        and row_count % 128 == 0
        and height % 128 == 0
        and (model_width // (dp_count * cores)) % height == 0
        and args[5].shape[3] % 128 == 0
        and -(-(model_width // cores) // args[5].shape[3]) * capacity <= height
    )
    return (aligned_local if whole_tiles else plain_local)(*args)


def solution(mesh):
    in_specs = (
        P(("expert", "dp"), None),
        P(("expert", "dp"), None),
        P(("expert", "dp"), None),
        P("expert", None, None, "cuts"),
        P("expert", None, "cuts"),
        P("expert", "dp", None, "cuts"),
        P("expert", "dp", None, "cuts"),
        P("expert", "dp", None, "cuts"),
        P(),
    )
    out_specs = (
        P(("expert", "dp"), "cuts"),
        P("expert", None, "dp", None, "cuts"),
        P("expert", None, "dp", None, "cuts"),
        P("expert", None, "dp", None, "cuts"),
    )
    return jax.shard_map(local, mesh=mesh, in_specs=in_specs, out_specs=out_specs, check_vma=False)
```
